256 devices in a mesh: pool: 2 (over y_lo), rank: 128 (over z, x, y_hi, core).
Axes of the slice: x: 4, y: 4 (y_hi: 2, y_lo: 2; y = y_hi * 2 + y_lo), z: 8, core: 2. Of those that a mesh axis runs over, the one named last changes fastest.
Arguments:
- queries: bfloat16 [256, 64, 256], P(('pool', 'rank'))
- cache_keys: bfloat16 [256, 2048, 256], P(('pool', 'rank'))
- cache_values: bfloat16 [256, 2048, 256], P(('pool', 'rank')), may hold values from -6 to 6
- new_keys: bfloat16 [256, 256], P(('pool', 'rank')), may hold values from -6 to 6
- new_values: bfloat16 [256, 256], P(('pool', 'rank')), may hold values from -6 to 6
- lengths: int32 [256], P(('pool', 'rank')), may hold values from 512 to 2048, as said below
- residual: bfloat16 [256, 7168], P('pool', 'rank'), may hold values from -4 to 4
- out_weight: bfloat16 [7168, 16384], P('rank'), may hold values from -0.375 to 0.375
- norm_gain: float32 [7168], replicated, may hold values from 0.5 to 1.5
- router_weight: bfloat16 [7168, 8], replicated, may hold values from -0.0625 to 0.0625
- routes: int32 [256, 3], replicated, may hold values from 0 to 7, all different within a row; in each aligned block of 256 rows (0 to 255, 256 to 511, ...) at most 160 rows name the same one
- gate_tiles: bfloat16 [256, 7168, 160], P(('pool', 'rank')), may hold values from -0.0625 to 0.0625
- up_tiles: bfloat16 [256, 7168, 160], P(('pool', 'rank')), may hold values from -0.0625 to 0.0625
- down_tiles: bfloat16 [256, 160, 7168], P(('pool', 'rank')), may hold values from -0.078125 to 0.078125
Outputs:
- output: bfloat16 [256, 7168], P('pool', 'rank')
The draws below stay inside these ranges and needn't reach their ends.
Inputs may be any that keep to these rules, and one draw needn't show every extreme that they name: `lengths`: some row's cache is full. `routes`: each row names 3 different experts; over all 256 rows no expert is named by more than 160 rows, a bound that some block reaches.
All inputs are finite; a program needn't handle non-finite values.
Results may differ from the reference program's by a relative error of at most 0.012.
Values may be sent and summed in bfloat16 or wider, within the bound.
A program may use at most 128 MiB of HBM per device.

```python
import math
import jax
import jax.numpy as jnp
import numpy as np
from jax import lax

D = 7168
HEADS = 64
HD = 256
HE = 5120
TOP = 3
EXPERTS = 8
CTX = 2048
ROWS = 256
TILES = 32
HT = 160
CAP = 160
DEVICES = 256


def shared_keys(key):
    base_keys = jnp.clip(jax.random.normal(key, (ROWS, CTX, HD), jnp.float32), -5.0, 5.0)
    return base_keys


def draw_cache_keys(key, part):
    base_keys = shared_keys(key)
    return base_keys.astype(jnp.bfloat16)


def draw_queries(key, part):
    key = jax.random.fold_in(key, 5)
    jitter = jax.random.normal(key, (ROWS, HEADS, HD), jnp.float32)
    return jitter.astype(jnp.bfloat16)


def draw_lengths(key, part):
    key = jax.random.fold_in(key, 13)
    sampled = jax.random.randint(key, (ROWS,), CTX // 4, CTX + 1)
    full_row = jax.random.randint(jax.random.fold_in(key, 1), (), 0, ROWS)
    return sampled.at[full_row].set(CTX).astype(jnp.int32)


def block_levels(stream_key, dims, cuts, least, top_value):
    level = 1.0
    for dim, parts in cuts:
        heights = jax.random.uniform(jax.random.fold_in(jax.random.fold_in(stream_key, 6), dim), (parts,), jnp.float32, least / len(cuts), top_value / len(cuts))
        level = level * jnp.repeat(jnp.exp(heights), dims[dim] // parts).reshape((-1,) + (1,) * (len(dims) - 1 - dim))
    return level


def routed_block(rng, own, number, rows, number_of, top, bound, slope):
    ranking = jax.random.permutation(rng, number_of)
    crowded, usual = load_shares(number_of, rows * top, bound, slope, True), load_shares(number_of, rows * top, bound, slope, False)
    places = jnp.arange(number_of)

    def named(sizes, offset_by):
        used = int((sizes > 0).sum())
        fixed = max(1, used // 4)
        moved = fixed + (places - fixed + offset_by * (used - fixed)) % max(1, number_of - fixed)
        return jnp.zeros((number_of,), jnp.int32).at[ranking[jnp.where(places < fixed, places, moved)]].set(jnp.asarray(sizes, jnp.int32))

    sizes = jnp.where(number % 4 == 0, named(crowded, number // 4), named(usual, number - number // 4 - 1))
    mixed = jax.random.permutation(jax.random.fold_in(own, 3), number_of)
    donor, receiver = mixed[0:number_of // 2 * 2:2], mixed[1:number_of // 2 * 2:2]
    slack = jnp.minimum(sizes[donor] - 1, bound - sizes[receiver]) // 2
    slack = jnp.where((donor == ranking[0]) | (receiver == ranking[0]) | (sizes[receiver] == 0), 0, jnp.maximum(slack, 0))
    moved = jax.random.randint(jax.random.fold_in(own, 4), (number_of // 2,), 0, 1 << 20) % (slack + 1)
    sizes = sizes.at[donor].add(-moved).at[receiver].add(moved)
    labels = jnp.searchsorted(jnp.cumsum(sizes), jnp.arange(rows * top), side="right").astype(jnp.int32)
    grid = labels.reshape(top, rows).T
    grid = grid[jax.random.permutation(jax.random.fold_in(own, 1), rows)]
    offset_by = jax.random.randint(jax.random.fold_in(own, 2), (rows, 1), 0, top)
    return jnp.take_along_axis(grid, (jnp.arange(top)[None, :] + offset_by) % top, axis=1)


def load_shares(amount, total, most, slope, full):
    portions = [(1 << 20) // math.isqrt(standing ** slope) + 1 for standing in range(1, amount + 1)]
    largest = most if full else min(most, max(-(-total // amount), total * portions[0] // sum(portions)))
    least = 1 if total - largest >= amount - 1 else 0
    given, spare = [largest] + [least] * (amount - 1), total - largest - least * (amount - 1)
    while spare > 0:
        movable = [i for i in range(1, amount) if given[i] < largest] or [i for i in range(1, amount) if given[i] < most]
        whole, budget = sum([portions[i] for i in movable]), spare
        for i in movable:
            addition = min(most - given[i], max(1, budget * portions[i] // whole), spare)
            given[i] = given[i] + addition
            spare = spare - addition
    return np.array(given)


def bell_draw(own_key, dims, deviation, limit, pieces=(), kind=jnp.bfloat16):
    drawn = deviation * jax.random.normal(own_key, dims, jnp.float32)
    if pieces:
        drawn = drawn * block_levels(own_key, dims, pieces, -0.22, 0.18)
    return jnp.clip(drawn, -limit, limit).astype(kind)


def setup_inputs(seed: int = 0) -> dict:
    splits = jax.random.split(jax.random.key(seed), 15)
    queries = draw_queries(jax.random.fold_in(splits[14], 71), 0)
    cache_keys = draw_cache_keys(jax.random.fold_in(splits[14], 71), 0)
    cache_values = bell_draw(splits[2], (ROWS, CTX, HD), 1.0, 6.0, ((0, 256),))
    new_keys = bell_draw(splits[3], (ROWS, HD), 1.0, 6.0, ((0, 256),))
    new_values = bell_draw(splits[4], (ROWS, HD), 1.0, 6.0, ((0, 256),))
    lengths = draw_lengths(jax.random.fold_in(splits[14], 71), 0)
    residual = bell_draw(splits[6], (ROWS, D), 0.3, 4.0, ((0, 2), (1, 128)))
    out_weight = bell_draw(splits[7], (D, HEADS * HD), HD ** -0.5, 0.375, ((0, 128),))
    norm_gain = jnp.clip(1.0 + 0.1 * jax.random.normal(splits[8], (D,), jnp.float32), 0.5, 1.5)
    router_weight = bell_draw(splits[9], (D, EXPERTS), D ** -0.5, 0.0625)
    routes_keys = jax.random.split(jax.random.fold_in(splits[10], 1), ROWS // ROWS)
    routes_turns = jax.random.permutation(jax.random.fold_in(splits[10], 3), ROWS // ROWS)
    routes = jax.vmap(lambda own, number: routed_block(jax.random.fold_in(splits[10], 2), own, number, ROWS, EXPERTS, TOP, CAP, 1))(routes_keys, routes_turns).reshape((ROWS, TOP))
    gate_tiles = bell_draw(splits[11], (DEVICES, D, HT), D ** -0.5, 0.0625, ((0, 256),))
    up_tiles = bell_draw(splits[12], (DEVICES, D, HT), D ** -0.5, 0.0625, ((0, 256),))
    down_tiles = bell_draw(splits[13], (DEVICES, HT, D), HE ** -0.5, 0.078125, ((0, 256),))
    return dict(queries=queries, cache_keys=cache_keys, cache_values=cache_values, new_keys=new_keys, new_values=new_values, lengths=lengths, residual=residual, out_weight=out_weight, norm_gain=norm_gain, router_weight=router_weight, routes=routes, gate_tiles=gate_tiles, up_tiles=up_tiles, down_tiles=down_tiles)


epsilon = 1e-05

def choose_rows(expert, routes, gate_share, capacity):
    matches = routes == expert
    member = jnp.any(matches, axis=1)
    slot_rows = jnp.argsort(jnp.where(member, 0, 1).astype(jnp.int32), stable=True)[:capacity].astype(jnp.int32)
    filled = jnp.sum(member.astype(jnp.int32))
    occupied = jnp.arange(capacity, dtype=jnp.int32) < filled
    shares = lax.optimization_barrier(jnp.sum(jnp.where(matches, gate_share, jnp.zeros_like(gate_share)), axis=1))[slot_rows]
    shares = jnp.where(occupied, shares, jnp.zeros_like(shares))
    return (slot_rows, shares, filled)

def attend_row(operands):
    query_row, keys_row, values_row, key_new, value_new, length = operands
    factor = query_row.shape[-1] ** (-0.5)
    scores = jnp.dot(query_row, keys_row.T, preferred_element_type=jnp.float32) * factor
    self_score = jnp.dot(query_row, key_new, preferred_element_type=jnp.float32) * factor
    visible = jnp.arange(keys_row.shape[0], dtype=jnp.int32) < length
    scores = jnp.where(visible[None, :], scores, -1e+30)
    highest = jnp.maximum(lax.optimization_barrier(jnp.max(scores, axis=1)), self_score)
    raised = jnp.exp(scores - highest[:, None])
    raised_self = jnp.exp(self_score - highest)
    denominator = lax.optimization_barrier(jnp.sum(raised, axis=1)) + raised_self
    weights_cache = (raised / denominator[:, None]).astype(jnp.bfloat16)
    weights_self = (raised_self / denominator).astype(jnp.bfloat16)
    context = jnp.dot(weights_cache, values_row, preferred_element_type=jnp.float32)
    context = context + weights_self.astype(jnp.float32)[:, None] * value_new.astype(jnp.float32)[None, :]
    return context.astype(jnp.bfloat16)

def reference(queries, cache_keys, cache_values, new_keys, new_values, lengths, residual, out_weight, norm_gain, router_weight, routes, gate_tiles, up_tiles, down_tiles):
    attended = lax.map(attend_row, (queries, cache_keys, cache_values, new_keys, new_values, lengths))
    attended = attended.reshape(ROWS, HEADS * HD)
    projected = jnp.dot(attended, out_weight.T, preferred_element_type=jnp.float32)
    hstate = (residual.astype(jnp.float32) + projected).astype(jnp.bfloat16)
    widened = hstate.astype(jnp.float32)
    mean_square = lax.optimization_barrier(jnp.mean(widened * widened, axis=1, keepdims=True))
    normed = (widened * lax.rsqrt(mean_square + epsilon) * norm_gain).astype(jnp.bfloat16)
    logits = jnp.dot(normed, router_weight, preferred_element_type=jnp.float32)
    chosen = jax.nn.sigmoid(jnp.take_along_axis(logits, routes, axis=1))
    gate_share = chosen / lax.optimization_barrier(jnp.sum(chosen, axis=1, keepdims=True))
    gate_full = gate_tiles.reshape(EXPERTS, TILES, D, HT).transpose(0, 2, 1, 3).reshape(EXPERTS, D, HE)
    up_full = up_tiles.reshape(EXPERTS, TILES, D, HT).transpose(0, 2, 1, 3).reshape(EXPERTS, D, HE)
    down_full = down_tiles.reshape(EXPERTS, HE, D)

    def add_expert(running, operands):
        expert, gate_matrix, up_matrix, down_matrix = operands
        slot_rows, shares, filled = choose_rows(expert, routes, gate_share, CAP)
        picked = normed[slot_rows]
        gate_part = jnp.dot(picked, gate_matrix, preferred_element_type=jnp.float32)
        up_part = jnp.dot(picked, up_matrix, preferred_element_type=jnp.float32)
        activated = (jax.nn.silu(gate_part) * up_part).astype(jnp.bfloat16)
        partial_value = jnp.dot(activated, down_matrix, preferred_element_type=jnp.float32) * shares[:, None]
        return (running.at[slot_rows].add(partial_value), None)
    routed_sum, unused = lax.scan(add_expert, jnp.zeros((ROWS, D), jnp.float32), (jnp.arange(EXPERTS, dtype=jnp.int32), gate_full, up_full, down_full))
    return (widened + routed_sum).astype(jnp.bfloat16)
```

```python
import jax
import jax.numpy as jnp
from jax import lax
from jax.experimental import pallas as pl
from jax.experimental.pallas import tpu as pltpu
from jax.sharding import PartitionSpec as P

MESH = pl.DeviceIdType.MESH
BF = jnp.bfloat16
F32 = jnp.float32
EPSILON = 1e-05
SLOTS = 160
WIDE = 112
VM = pl.BlockSpec(memory_space=pltpu.VMEM)
ANY = pl.BlockSpec(memory_space=pl.ANY)


def place(rank):
    return rank // 16, lax.rem(rank // 4, 4), lax.rem(rank // 2, 2), lax.rem(rank, 2)


def rank_of(z, x, yh, c):
    return z * 16 + x * 4 + yh * 2 + c


def iota(shape, dim):
    return lax.broadcasted_iota(jnp.int32, shape, dim)


def dot(a, b):
    return jnp.dot(a, b, preferred_element_type=F32)


def wait_bytes(ref, sem):
    pltpu.make_async_copy(ref, ref, sem).wait()


def gather_kernel(
    att, residual, weight_hbm, h_ref, plane, rows, weight, w_sem, own_sem, p_send, p_recv, up_send,
    up_recv, down_send, down_recv, core_send, core_recv,
):
    pool, rank = lax.axis_index("pool"), lax.axis_index("rank")
    z, x, yh, c = place(rank)
    mine = lax.rem(rank, 16)
    sibling = rank + 1 - 2 * c
    up = rank_of(lax.rem(z + 1, 8), x, yh, c)
    down = rank_of(lax.rem(z + 7, 8), x, yh, c)

    def at(r):
        return (pool, r)

    barrier = pltpu.get_barrier_semaphore()

    def greet(d, _):
        r = z * 16 + lax.rem(mine + d, 16)
        pl.semaphore_signal(barrier, inc=1, device_id=at(r), device_id_type=MESH)
        return 0

    lax.fori_loop(1, 16, greet, 0)
    pl.semaphore_signal(barrier, inc=1, device_id=at(up), device_id_type=MESH)
    pl.semaphore_signal(barrier, inc=1, device_id=at(down), device_id_type=MESH)
    load = pltpu.make_async_copy(weight_hbm, weight, w_sem)
    load.start()
    own = pltpu.make_async_copy(att, plane.at[mine], own_sem)
    own.start()
    pl.semaphore_wait(barrier, 17)

    def to_plane(d, _):
        r = z * 16 + lax.rem(mine + d, 16)
        pltpu.make_async_remote_copy(
            src_ref=att, dst_ref=plane.at[mine], send_sem=p_send, recv_sem=p_recv,
            device_id=at(r), device_id_type=MESH,
        ).start()
        return 0

    lax.fori_loop(1, 16, to_plane, 0)
    own.wait()
    wait_bytes(plane.at[pl.ds(0, 15)], p_recv)

    def turn(k, _):
        part = plane[:, pl.ds(pl.multiple_of(k * 16, 16), 16), :]
        part = jnp.swapaxes(part, 0, 1)
        for s in range(16):
            rows[z, :, pl.ds(pl.multiple_of((k * 16 + s) * 128, 128), 128)] = part[s]
        return 0

    lax.fori_loop(0, 8, turn, 0)

    half = pl.multiple_of(c * 8192, 128)

    def block(b, start, size):
        return rows.at[b, :, pl.ds(pl.multiple_of(half + start, 128), size)]

    def ring(b, start, size, to, send, recv):
        return pltpu.make_async_remote_copy(
            src_ref=block(b, start, size), dst_ref=block(b, start, size), send_sem=send,
            recv_sem=recv, device_id=at(to), device_id_type=MESH,
        )

    def share(b):
        pltpu.make_async_remote_copy(
            src_ref=block(b, 0, 8192), dst_ref=block(b, 0, 8192), send_sem=core_send,
            recv_sem=core_recv, device_id=at(sibling), device_id_type=MESH,
        ).start()

    for s in range(4):
        b_up, b_down = lax.rem(z + 8 - s, 8), lax.rem(z + s, 8)
        size = 8192 if s < 3 else 4096
        a = ring(b_up, 0, size, up, up_send.at[s], up_recv.at[s])
        b = ring(b_down, 8192 - size, size, down, down_send.at[s], down_recv.at[s])
        a.start()
        b.start()
        a.wait()
        b.wait()
        if s < 3:
            share(lax.rem(z + 7 - s, 8))
            share(lax.rem(z + 1 + s, 8))
        else:
            share(lax.rem(z + 4, 8))
    wait_bytes(plane.at[pl.ds(0, 15)], p_send)
    seven = rows.at[pl.ds(0, 7), :, pl.ds(0, 8192)]
    wait_bytes(seven, core_send)
    wait_bytes(seven, core_recv)
    load.wait()
    total = lax.dot_general(
        rows[...].reshape(128, 16384), weight[...], (((1,), (1,)), ((), ())),
        preferred_element_type=F32,
    )
    h_ref[...] = (residual[...].astype(F32) + total).astype(BF)


def expert_kernel(
    h_ref, routes_ref, routes_t_ref, gain_ref, router_ref, gate_hbm, up_hbm, down_hbm, out_ref,
    states, merged, outgoing, slot_in, gathered, normed, gate, up, down_in, down, partial,
    from_core, to_group, from_group, to_rows, from_experts, acc_g, acc_u, acc_r, counts, pick_t,
    w_sem, m_send, m_recv, b_send, b_recv, g_send, g_recv, s_send, s_recv, c_send, c_recv, r_send,
    r_recv, d_send, d_recv,
):
    pool, rank = lax.axis_index("pool"), lax.axis_index("rank")
    z, x, yh, c = place(rank)
    zb = lax.rem(z, 2)
    expert = pool * 4 + z // 2
    spot = zb * 8 + x * 2 + yh
    sibling = rank + 1 - 2 * c

    def member(spot_of, core):
        return (z // 2) * 32 + spot_of * 2 + core

    def pair_of(core, spot_of, i):
        return (4 * (spot_of // 8) + 2 * core + i) * 8 + lax.rem(spot_of, 8)

    def copy(src, dst, send, recv, p, r):
        return pltpu.make_async_remote_copy(
            src_ref=src, dst_ref=dst, send_sem=send, recv_sem=recv, device_id=(p, r),
            device_id_type=MESH,
        )

    zero16 = jnp.zeros((16, SLOTS), BF)

    def load(t, _):
        core, g, i = t // 32, lax.rem(t // 2, 16), lax.rem(t, 2)
        start = pl.multiple_of(pair_of(core, g, i) * WIDE, 16)
        base = pl.multiple_of(t * 128, 128)
        for src, dst in ((gate_hbm, gate), (up_hbm, up)):
            pltpu.make_async_copy(
                src.at[0, pl.ds(start, WIDE), :], dst.at[pl.ds(base, WIDE), :], w_sem.at[0]
            ).start()
        gate[pl.ds(base + WIDE, 16), :] = zero16
        up[pl.ds(base + WIDE, 16), :] = zero16
        return 0

    barrier = pltpu.get_barrier_semaphore()

    def greet(p, r):
        here = jnp.logical_and(p == pool, r == rank)

        @pl.when(jnp.logical_not(here))
        def _():
            pl.semaphore_signal(barrier, inc=1, device_id=(p, r), device_id_type=MESH)

    greet(pool, sibling)
    greet(1 - pool, rank)
    greet(1 - pool, sibling)
    for i in range(2):
        greet(pool, rank_of(4 * zb + 2 * c + i, x, yh, (z // 2) // 2))

    def greet_group(d, _):
        greet(pool, member(lax.rem(spot + d, 16), c))
        return 0

    lax.fori_loop(1, 16, greet_group, 0)

    def greet_sums(e, _):
        greet(e // 4, rank_of(2 * lax.rem(e, 4) + z // 4, x, yh, lax.rem(z // 2, 2)))
        return 0

    lax.fori_loop(0, 8, greet_sums, 0)
    pltpu.make_async_copy(
        down_hbm.at[0], down_in.at[:, pl.ds(0, 7168)], w_sem.at[1]
    ).start()
    lax.fori_loop(0, 64, load, 0)
    down_in[:, pl.ds(7168, 128)] = jnp.zeros((SLOTS, 128), BF)

    shift = (iota((56, 128), 0) + 56 * c == iota((56, 128), 1)).astype(BF)
    states[pool, c] = dot(h_ref[...], shift).astype(BF)

    routes = routes_ref[...]
    lanes8 = iota((256, 8), 1)
    member_t = jnp.zeros((256, 8), F32)
    for k in range(3):
        member_t += (routes[:, k : k + 1] == lanes8).astype(F32)
    member_n = jnp.zeros((8, 256), F32)
    rows8 = iota((8, 256), 0)
    for k in range(3):
        member_n += (routes_t_ref[k : k + 1, :] == rows8).astype(F32)
    r0, r1 = iota((256, 256), 0), iota((256, 256), 1)
    place_n = dot(member_n.astype(BF), (r0 < r1).astype(BF))
    place_t = dot((r1 < r0).astype(BF), member_t.astype(BF))
    counts[...] = jnp.where(member_n > 0.5, place_n, -1.0)
    column = jnp.sum(
        jnp.where(lanes8 == expert, jnp.where(member_t > 0.5, place_t, -1.0), 0.0), axis=1,
        keepdims=True,
    )
    pick_t[...] = (column == iota((256, SLOTS), 1).astype(F32)).astype(BF)

    def pick(e):
        return (counts[pl.ds(e, 1), :] == iota((SLOTS, 256), 0).astype(F32)).astype(BF)

    same = jnp.logical_and(z // 4 == zb, lax.rem(z // 2, 2) == c)
    self_sums = same.astype(jnp.int32)
    self_slots = jnp.logical_and(same, zb == c).astype(jnp.int32)
    pl.semaphore_wait(barrier, 28 - self_sums - self_slots)

    partners = ((pool, sibling), (1 - pool, rank), (1 - pool, sibling))
    sent = []
    for n, (p, r) in enumerate(partners):
        put = copy(states.at[pool, c], states.at[pool, c], m_send.at[n], m_recv.at[n], p, r)
        put.start()
        sent.append(put)
    for put in sent:
        put.wait()
    for p in range(2):
        merged[p * 128 : p * 128 + 128, :] = states[p, 0] + states[p, 1]

    for i in range(2):
        outgoing[i] = dot(pick(pool * 4 + 2 * c + i), merged[...]).astype(BF)
    for i in range(2):
        r = rank_of(2 * (2 * c + i) + z // 4, x, yh, lax.rem(z // 2, 2))
        src, dst = outgoing.at[i], slot_in.at[lax.rem(z, 2)]

        @pl.when(r == rank)
        def _():
            pltpu.make_async_copy(src, dst, b_recv.at[lax.rem(z, 2)]).start()

        @pl.when(r != rank)
        def _():
            copy(src, dst, b_send.at[i], b_recv.at[lax.rem(z, 2)], pool, r).start()

    for i in range(2):
        wait_bytes(slot_in.at[i], b_recv.at[i])

    mine = gathered.at[c, spot]
    own = pltpu.make_async_copy(slot_in, mine, w_sem.at[2])
    own.start()

    def to_group_start(d, _):
        to = lax.rem(spot + d, 16)
        copy(slot_in, mine, g_send, g_recv.at[spot], pool, member(to, c)).start()
        return 0

    lax.fori_loop(1, 16, to_group_start, 0)
    own.wait()
    copy(slot_in, mine, s_send, s_recv, pool, sibling).start()

    def pass_on(d, _):
        frm = lax.rem(spot + d, 16)
        wait_bytes(gathered.at[c, frm], g_recv.at[frm])
        copy(
            gathered.at[c, frm], gathered.at[c, frm], s_send, s_recv, pool, sibling
        ).start()
        return 0

    lax.fori_loop(1, 16, pass_on, 0)

    wait_bytes(down_hbm.at[0], w_sem.at[1])

    def cut(t, _):
        core, g, i = t // 32, lax.rem(t // 2, 16), lax.rem(t, 2)
        start = pair_of(core, g, i) * WIDE
        window = down_in[:, pl.ds(pl.multiple_of(start // 128 * 128, 128), 256)]
        a, b = iota((256, 128), 0), iota((256, 128), 1)
        shift = jnp.logical_and(a == b + lax.rem(start, 128), b < WIDE).astype(BF)
        down[t] = dot(window, shift).astype(BF)
        return 0

    lax.fori_loop(0, 64, cut, 0)
    wait_bytes(gathered.at[0], s_recv)

    def squares(t, total):
        v = gathered[t // 32, lax.rem(t // 2, 16), lax.rem(t, 2)].astype(F32)
        return total + v * v

    total = lax.fori_loop(0, 64, squares, jnp.zeros((SLOTS, 128), F32))
    inv = lax.rsqrt(jnp.sum(total, axis=1, keepdims=True) * (1.0 / 7168) + EPSILON)

    def norm(t, _):
        core, g, i = t // 32, lax.rem(t // 2, 16), lax.rem(t, 2)
        v = gathered[core, g, i].astype(F32)
        scaled = v * inv * gain_ref[pl.ds(pair_of(core, g, i), 1), :]
        normed[:, pl.ds(pl.multiple_of(t * 128, 128), 128)] = scaled.astype(BF)
        return 0

    lax.fori_loop(0, 64, norm, 0)

    acc_g[...] = jnp.zeros_like(acc_g)
    acc_u[...] = jnp.zeros_like(acc_u)
    acc_r[...] = jnp.zeros_like(acc_r)
    all_w = gate_hbm.at[0]
    wait_bytes(all_w, w_sem.at[0])
    wait_bytes(all_w, w_sem.at[0])

    def multiply(u, _):
        k = pl.ds(pl.multiple_of(u * 1024, 1024), 1024)
        left = normed[:, k]
        acc_g[...] += dot(left, gate[k, :])
        acc_u[...] += dot(left, up[k, :])
        acc_r[...] += dot(left, router_ref[k, :])
        return 0

    lax.fori_loop(0, 8, multiply, 0)
    chosen = jax.nn.sigmoid(acc_r[...])
    named = dot(pick(expert), member_t.astype(BF))
    whole = jnp.sum(chosen * named, axis=1, keepdims=True)
    own_share = jnp.sum(jnp.where(iota((SLOTS, 8), 1) == expert, chosen * named, 0.0), axis=1, keepdims=True)
    filled = jnp.sum(named, axis=1, keepdims=True) > 0.5
    share = jnp.where(filled, own_share / jnp.where(filled, whole, 1.0), 0.0)
    hidden = (jax.nn.silu(acc_g[...]) * acc_u[...]).astype(BF)

    def product(core, n):
        t = core * 32 + n
        partial[core, n // 2, lax.rem(n, 2)] = (dot(hidden, down[t]) * share).astype(BF)

    def other_half(n, _):
        product(1 - c, n)
        return 0

    lax.fori_loop(0, 32, other_half, 0)
    swap = copy(partial.at[1 - c], from_core, c_send, c_recv, pool, sibling)
    swap.start()

    def own_half(n, _):
        product(c, n)
        return 0

    lax.fori_loop(0, 32, own_half, 0)
    swap.wait()

    def chip_sum(d, _):
        to = lax.rem(spot + d, 16)
        to_group[to] = (partial[c, to].astype(F32) + from_core[to].astype(F32)).astype(BF)
        copy(
            to_group.at[to], from_group.at[spot], r_send, r_recv, pool, member(to, c)
        ).start()
        return 0

    lax.fori_loop(1, 16, chip_sum, 0)
    from_group[spot] = (partial[c, spot].astype(F32) + from_core[spot].astype(F32)).astype(BF)
    wait_bytes(from_group.at[pl.ds(0, 15)], r_recv)

    for i in range(2):
        def add(s, total):
            return total + from_group[s, i].astype(F32)

        total = lax.fori_loop(0, 16, add, jnp.zeros((SLOTS, 128), F32))
        spread = dot(pick_t[...], total.astype(BF)).astype(BF)
        for p in range(2):
            to_rows[i, p] = spread[p * 128 : p * 128 + 128, :]
        for p in range(2):
            for core in range(2):
                r = rank_of(4 * zb + 2 * c + i, x, yh, core)
                src, dst = to_rows.at[i, p], from_experts.at[expert]
                here = jnp.logical_and(pool == p, r == rank)

                @pl.when(here)
                def _():
                    pltpu.make_async_copy(src, dst, d_recv).start()

                @pl.when(jnp.logical_not(here))
                def _():
                    copy(src, dst, d_send, d_recv, p, r).start()

    wait_bytes(from_experts, d_recv)
    sums = jnp.zeros((128, 128), F32)
    for e in range(8):
        sums += from_experts[e].astype(F32)
    back = (iota((128, 56), 0) == iota((128, 56), 1) + 56 * c).astype(F32)
    mine_sum = jnp.dot(sums, back, preferred_element_type=F32, precision=lax.Precision.HIGHEST)
    out_ref[...] = (h_ref[...].astype(F32) + mine_sum).astype(BF)

    for i in range(2):
        r = rank_of(2 * (2 * c + i) + z // 4, x, yh, lax.rem(z // 2, 2))

        @pl.when(r != rank)
        def _():
            wait_bytes(outgoing.at[i], b_send.at[i])

    wait_bytes(gathered.at[0, pl.ds(0, 15)], g_send)
    wait_bytes(gathered.at[0], s_send)
    wait_bytes(from_group.at[pl.ds(0, 15)], r_send)
    wait_bytes(from_experts.at[pl.ds(0, 7)], d_send)

    @pl.when(jnp.logical_not(same))
    def _():
        wait_bytes(from_experts.at[0], d_send)


def attention(queries, cache_keys, cache_values, new_keys, new_values, lengths):
    factor = queries.shape[-1] ** (-0.5)
    scores = jnp.einsum("rhd,rcd->rhc", queries, cache_keys, preferred_element_type=F32) * factor
    self_score = jnp.einsum("rhd,rd->rh", queries, new_keys, preferred_element_type=F32) * factor
    visible = jnp.arange(cache_keys.shape[1], dtype=jnp.int32)[None, None, :] < lengths[:, None, None]
    scores = jnp.where(visible, scores, -1e30)
    highest = jnp.maximum(jnp.max(scores, axis=2), self_score)
    raised = jnp.exp(scores - highest[:, :, None])
    raised_self = jnp.exp(self_score - highest)
    denominator = jnp.sum(raised, axis=2) + raised_self
    weights_cache = (raised / denominator[:, :, None]).astype(BF)
    weights_self = (raised_self / denominator).astype(BF)
    context = jnp.einsum("rhc,rcd->rhd", weights_cache, cache_values, preferred_element_type=F32)
    context = context + weights_self.astype(F32)[:, :, None] * new_values.astype(F32)[:, None, :]
    return context.astype(BF)


def local(
    queries, cache_keys, cache_values, new_keys, new_values, lengths, residual, out_weight,
    norm_gain, router_weight, routes, gate_tiles, up_tiles, down_tiles,
):
    attended = attention(queries, cache_keys, cache_values, new_keys, new_values, lengths)
    dma = pltpu.SemaphoreType.DMA
    hstate = pl.pallas_call(
        gather_kernel,
        out_shape=jax.ShapeDtypeStruct((128, 56), BF),
        in_specs=[VM, VM, ANY],
        out_specs=VM,
        scratch_shapes=[
            pltpu.VMEM((16, 128, 128), BF),
            pltpu.VMEM((8, 16, 16384), BF),
            pltpu.VMEM((56, 16384), BF),
            dma, dma, dma, dma, dma((4,)), dma((4,)), dma((4,)), dma((4,)), dma, dma,
        ],
        compiler_params=pltpu.CompilerParams(
            collective_id=0, has_side_effects=True, vmem_limit_bytes=48 * 2**20
        ),
        name="gather_project",
    )(attended.reshape(128, 128), residual, out_weight)
    gain = jnp.pad(norm_gain.reshape(64, WIDE), ((0, 0), (0, 16)))
    router = jnp.pad(router_weight.reshape(64, WIDE, 8), ((0, 0), (0, 16), (0, 0)))
    router = router.reshape(2, 2, 2, 8, 128, 8).transpose(1, 0, 3, 2, 4, 5).reshape(8192, 8)
    return pl.pallas_call(
        expert_kernel,
        out_shape=jax.ShapeDtypeStruct((128, 56), BF),
        in_specs=[VM, VM, VM, VM, VM, ANY, ANY, ANY],
        out_specs=VM,
        scratch_shapes=[
            pltpu.VMEM((2, 2, 128, 128), BF),
            pltpu.VMEM((256, 128), BF),
            pltpu.VMEM((2, SLOTS, 128), BF),
            pltpu.VMEM((2, SLOTS, 128), BF),
            pltpu.VMEM((2, 16, 2, SLOTS, 128), BF),
            pltpu.VMEM((SLOTS, 8192), BF),
            pltpu.VMEM((8192, SLOTS), BF),
            pltpu.VMEM((8192, SLOTS), BF),
            pltpu.VMEM((SLOTS, 7296), BF),
            pltpu.VMEM((64, SLOTS, 128), BF),
            pltpu.VMEM((2, 16, 2, SLOTS, 128), BF),
            pltpu.VMEM((16, 2, SLOTS, 128), BF),
            pltpu.VMEM((16, 2, SLOTS, 128), BF),
            pltpu.VMEM((16, 2, SLOTS, 128), BF),
            pltpu.VMEM((2, 2, 128, 128), BF),
            pltpu.VMEM((8, 128, 128), BF),
            pltpu.VMEM((SLOTS, SLOTS), F32),
            pltpu.VMEM((SLOTS, SLOTS), F32),
            pltpu.VMEM((SLOTS, 8), F32),
            pltpu.VMEM((8, 256), F32),
            pltpu.VMEM((256, SLOTS), BF),
            dma((3,)), dma((3,)), dma((3,)), dma((2,)), dma((2,)), dma, dma((16,)), dma, dma, dma,
            dma, dma, dma, dma, dma,
        ],
        compiler_params=pltpu.CompilerParams(
            collective_id=1, has_side_effects=True, vmem_limit_bytes=56 * 2**20
        ),
        name="experts",
    )(hstate, routes, routes.T, gain, router, gate_tiles, up_tiles, down_tiles)


def solution(mesh):
    return jax.shard_map(
        local,
        mesh=mesh,
        in_specs=(
            P(("pool", "rank"), None, None),
            P(("pool", "rank"), None, None),
            P(("pool", "rank"), None, None),
            P(("pool", "rank"), None),
            P(("pool", "rank"), None),
            P(("pool", "rank")),
            P("pool", "rank"),
            P("rank", None),
            P(),
            P(),
            P(),
            P(("pool", "rank"), None, None),
            P(("pool", "rank"), None, None),
            P(("pool", "rank"), None, None),
        ),
        out_specs=P("pool", "rank"),
        check_vma=False,
    )
```

```python
import jax
import jax.numpy as jnp
from jax import lax
from jax.experimental import pallas as pl
from jax.experimental.pallas import tpu as pltpu
from jax.sharding import PartitionSpec as P

MESH = pl.DeviceIdType.MESH
BF = jnp.bfloat16
F32 = jnp.float32
EPSILON = 1e-05
SLOTS = 160
WIDE = 112
VM = pl.BlockSpec(memory_space=pltpu.VMEM)
ANY = pl.BlockSpec(memory_space=pl.ANY)


def place(rank):
    return rank // 16, lax.rem(rank // 4, 4), lax.rem(rank // 2, 2), lax.rem(rank, 2)


def rank_of(z, x, yh, c):
    return z * 16 + x * 4 + yh * 2 + c


def iota(shape, dim):
    return lax.broadcasted_iota(jnp.int32, shape, dim)


def dot(a, b):
    return jnp.dot(a, b, preferred_element_type=F32)


def wait_bytes(ref, sem):
    pltpu.make_async_copy(ref, ref, sem).wait()


def padded(tiles):
    out = []
    for j in range(8):
        parts = []
        if j > 0:
            parts.append(tiles[j - 1][:, 128 - 16 * j :])
        if j < 7:
            parts.append(tiles[j][:, : WIDE - 16 * j])
        parts.append(jnp.zeros((tiles[0].shape[0], 16), tiles[0].dtype))
        out.append(jnp.concatenate([part for part in parts if part.shape[1]], axis=1))
    return out


def lane_tile(n):
    return pl.ds(pl.multiple_of(n * 128, 128), 128)


def layer_kernel(
    queries_hbm, keys_hbm, values_hbm, new_key_ref, new_value_ref, length_ref, residual_hbm,
    weight_hbm, gain_ref, router_ref, routes_ref, gate_hbm, up_hbm, down_hbm, out_ref,
    queries, keys, values, residual, weight, gate, up, down, fused, cut, rows_in, rows, states_in,
    state_sent, states, acc, partial, from_core, to_group, from_group, to_rows, from_experts,
    places, load_sem, a_plane, a_plane_in, a_ring, a_up_in, a_down_in, a_core, a_core_in, b_plane,
    b_plane_in, b_ring, b_up_in, b_down_in, b_core, b_core_in, m_send, m_recv, c_send, c_recv,
    r_send, r_recv, d_send, d_recv,
):
    pool, rank = lax.axis_index("pool"), lax.axis_index("rank")
    z, x, yh, c = place(rank)
    zb = lax.rem(z, 2)
    expert = pool * 4 + z // 2
    spot = zb * 8 + x * 2 + yh
    sibling = rank + 1 - 2 * c
    up_rank = rank_of(lax.rem(z + 1, 8), x, yh, c)
    down_rank = rank_of(lax.rem(z + 7, 8), x, yh, c)
    across = (pool == c).astype(jnp.int32)
    same = jnp.logical_and(z // 4 == zb, lax.rem(z // 2, 2) == c)

    def member(spot_of, core):
        return (z // 2) * 32 + spot_of * 2 + core

    def copy(src, dst, send, recv, p, r):
        return pltpu.make_async_remote_copy(
            src_ref=src, dst_ref=dst, send_sem=send, recv_sem=recv, device_id=(p, r),
            device_id_type=MESH,
        )

    def is_self(p, r):
        return jnp.logical_and(p == pool, r == rank)

    loads = []
    for n, (src, dst) in enumerate((
        (queries_hbm.at[0], queries), (keys_hbm.at[0], keys), (values_hbm.at[0], values),
        (residual_hbm, residual), (weight_hbm, weight), (gate_hbm.at[0], gate),
        (up_hbm.at[0], up), (down_hbm.at[0], down),
    )):
        load = pltpu.make_async_copy(src, dst, load_sem.at[n])
        load.start()
        loads.append(load)

    barrier = pltpu.get_barrier_semaphore()

    def greet(p, r):
        @pl.when(jnp.logical_not(is_self(p, r)))
        def _():
            pl.semaphore_signal(barrier, inc=1, device_id=(p, r), device_id_type=MESH)

    def greet_plane(d, _):
        greet(pool, z * 16 + lax.rem(x * 2 + yh + d, 8) * 2 + c)
        return 0

    def greet_group(d, _):
        greet(pool, member(lax.rem(spot + d, 16), c))
        return 0

    def greet_sums(e, _):
        greet(e // 4, rank_of(2 * lax.rem(e, 4) + z // 4, x, yh, lax.rem(z // 2, 2)))
        return 0

    lax.fori_loop(1, 8, greet_plane, 0)
    greet(pool, sibling)
    greet(pool, up_rank)
    greet(pool, down_rank)
    for core in range(2):
        greet(c, rank - c + core)
    lax.fori_loop(1, 16, greet_group, 0)
    lax.fori_loop(0, 8, greet_sums, 0)

    loads[0].wait()
    loads[1].wait()
    q = queries[...]
    scores = lax.dot_general(
        q, keys[...], (((1,), (1,)), ((), ())), preferred_element_type=F32
    ) * (1.0 / 16.0)
    self_score = jnp.sum(
        q.astype(F32) * new_key_ref[...].astype(F32), axis=1, keepdims=True
    ) * (1.0 / 16.0)
    scores = jnp.where(iota((64, 2048), 1) < length_ref[0], scores, -1e30)
    highest = jnp.maximum(jnp.max(scores, axis=1, keepdims=True), self_score)
    raised = jnp.exp(scores - highest)
    raised_self = jnp.exp(self_score - highest)
    denominator = jnp.sum(raised, axis=1, keepdims=True) + raised_self
    weights = (raised / denominator).astype(BF)
    weight_self = (raised_self / denominator).astype(BF).astype(F32)
    loads[2].wait()
    context = dot(weights, values[...]) + weight_self * new_value_ref[...].astype(F32)
    context = context.astype(BF)
    rows_in[z, x, yh, c, 0:64, :] = context[:, 0:128]
    rows_in[z, x, yh, c, 64:128, :] = context[:, 128:256]

    pl.semaphore_wait(barrier, 35 - across - same.astype(jnp.int32))

    def gather(buf, plane, plane_in, ring, up_in, down_in, core_send, core_in, work):
        own = buf.at[z, x, yh, c]
        flat = x * 2 + yh

        def to_plane(d, _):
            r = z * 16 + lax.rem(flat + d, 8) * 2 + c
            copy(own, own, plane, plane_in.at[flat], pool, r).start()
            return 0

        lax.fori_loop(1, 8, to_plane, 0)
        work(-1)

        def landed(d, _):
            j = lax.rem(flat + d, 8)
            wait_bytes(buf.at[z, j // 2, lax.rem(j, 2), c], plane_in.at[j])
            return 0

        lax.fori_loop(1, 8, landed, 0)

        def chunk(b, k):
            return buf.at[b, pl.ds(2 * k, 2), :, c]

        def share(b, k):
            copy(chunk(b, k), chunk(b, k), core_send, core_in.at[b], pool, sibling).start()

        for s in range(5):
            b_up, b_down = lax.rem(z + 8 - s, 8), lax.rem(z + s, 8)
            for k in range(2):
                if s > 0 and (s < 4 or k == 0):
                    wait_bytes(chunk(b_up, k), up_in.at[s - 1, k])
                if s < 3 or (s == 3 and k == 0):
                    copy(chunk(b_up, k), chunk(b_up, k), ring.at[0], up_in.at[s, k], pool, up_rank).start()
                if s > 0 and (s < 4 or k == 1):
                    wait_bytes(chunk(b_down, k), down_in.at[s - 1, k])
                if s < 3 or (s == 3 and k == 1):
                    copy(chunk(b_down, k), chunk(b_down, k), ring.at[1], down_in.at[s, k], pool, down_rank).start()
                if s < 4 or k == 0:
                    share(b_up, k)
                if 0 < s < 4 or (s == 4 and k == 1):
                    share(b_down, k)
            work(s)
        seven = buf.at[pl.ds(0, 7), pl.ds(0, 2), :, c]
        wait_bytes(buf.at[pl.ds(0, 7), 0, 0, c], plane)
        wait_bytes(seven, ring.at[0])
        wait_bytes(seven, ring.at[1])
        wait_bytes(buf.at[:, :, :, c], core_send)

    def from_sibling(buf, core_in, b):
        wait_bytes(buf.at[b, :, :, c], core_in.at[b])

    def step_planes(s):
        if s in (0, 4):
            return [lax.rem(z + s, 8)]
        return [lax.rem(z + 8 - s, 8), lax.rem(z + s, 8)]

    def prepare(b, _):
        gains = padded([gain_ref[:, lane_tile(b * 7 + j)] for j in range(7)])
        routers = padded([router_ref[:, lane_tile(b * 7 + j)].astype(F32) for j in range(7)])
        for j in range(8):
            part = (routers[j] * gains[j]).astype(BF)
            fused[320:336, lane_tile(b * 8 + j)] = jnp.concatenate([part, jnp.zeros_like(part)], axis=0)

        def strip(n, _):
            r = pl.ds(pl.multiple_of(n * 32, 32), 32)
            for src, first in ((gate, 0), (up, SLOTS)):
                tiles = padded([src[r, lane_tile(b * 7 + j)] for j in range(7)])
                to = pl.ds(pl.multiple_of(first + n * 32, 32), 32)
                for j in range(8):
                    fused[to, lane_tile(b * 8 + j)] = (tiles[j].astype(F32) * gains[j]).astype(BF)
            tiles = padded([down[r, lane_tile(b * 7 + j)] for j in range(7)])
            for j in range(8):
                cut[r, lane_tile(b * 8 + j)] = tiles[j]
            return 0

        lax.fori_loop(0, 5, strip, 0)
        return 0

    def turn(b):
        def part(k, _):
            block = rows_in[b, :, :, :, pl.ds(pl.multiple_of(k * 16, 16), 16), :]
            block = jnp.swapaxes(block.reshape(16, 16, 128), 0, 1)
            for j in range(16):
                n = 2 * (lax.rem(k, 4) * 16 + j) + k // 4
                rows[b, :, lane_tile(n)] = block[j]
            return 0

        lax.fori_loop(0, 8, part, 0)

    def row_work(s):
        if s < 0:
            return
        if s == 0:
            for load in loads[5:]:
                load.wait()
        if s < 4:
            lax.fori_loop(2 * s, 2 * s + 2, prepare, 0)
        for b in step_planes(s):
            from_sibling(rows_in, a_core_in, b)
            turn(b)

    gather(rows_in, a_plane, a_plane_in, a_ring, a_up_in, a_down_in, a_core, a_core_in, row_work)

    loads[3].wait()
    loads[4].wait()
    projected = lax.dot_general(
        rows[...].reshape(128, 16384), weight[...], (((1,), (1,)), ((), ())),
        preferred_element_type=F32,
    )
    hstate = (residual[...].astype(F32) + projected).astype(BF)

    shift = (iota((56, 128), 0) + 56 * c == iota((56, 128), 1)).astype(BF)
    state_sent[...] = dot(hstate, shift).astype(BF)
    for p in range(2):
        r = rank - c + pool
        here = is_self(p, r)

        @pl.when(here)
        def _():
            pltpu.make_async_copy(state_sent, states_in.at[c], m_recv.at[c]).start()

        @pl.when(jnp.logical_not(here))
        def _():
            copy(state_sent, states_in.at[c], m_send, m_recv.at[c], p, r).start()

    rows8 = iota((8, 256), 0)
    members = jnp.zeros((8, 256), F32)
    for k in range(3):
        members += (routes_ref[k : k + 1, :] == rows8).astype(F32)
    r0, r1 = iota((256, 256), 0), iota((256, 256), 1)
    order = dot(members.astype(BF), (r0 < r1).astype(BF))
    places[...] = jnp.where(members > 0.5, order, -1.0)
    own_places = places[pl.ds(expert, 1), :]
    picked = own_places == iota((SLOTS, 256), 0).astype(F32)
    pick = picked.astype(BF)
    acc[...] = jnp.zeros_like(acc)
    for i in range(2):
        wait_bytes(state_sent, m_recv.at[i])
    states[z, x, yh, c] = states_in[0] + states_in[1]

    def state_work(s):
        if s < 0:
            return
        for b in step_planes(s):
            from_sibling(states, b_core_in, b)
            halves = []
            for core in range(2):
                halves.append(jnp.concatenate(
                    [states[b, i // 2, i % 2, core] for i in range(8)], axis=1
                ))
            plane = jnp.concatenate(halves, axis=0)
            wide = plane.astype(F32)
            k = pl.ds(pl.multiple_of(b * 1024, 1024), 1024)
            product = lax.dot_general(
                fused[:, k], plane, (((1,), (1,)), ((), ())), preferred_element_type=F32
            )
            acc[0:336, :] += product
            square = wide * wide
            lanes = square[:, 0:128]
            for i in range(1, 8):
                lanes += square[:, i * 128 : i * 128 + 128]
            acc[336:344, :] += lax.dot_general(
                jnp.ones((8, 128), F32), lanes, (((1,), (1,)), ((), ())),
                preferred_element_type=F32, precision=lax.Precision.HIGHEST,
            )

    gather(states, b_plane, b_plane_in, b_ring, b_up_in, b_down_in, b_core, b_core_in, state_work)

    inv = lax.rsqrt(acc[336:337, :] * (1.0 / 7168) + EPSILON)
    chosen = jax.nn.sigmoid(acc[320:328, :] * inv)
    named = jnp.where(members > 0.5, chosen, 0.0)
    whole = jnp.sum(named, axis=0, keepdims=True)
    row_share = jnp.sum(jnp.where(rows8 == expert, named, 0.0), axis=0, keepdims=True) / whole
    hidden_t = (jax.nn.silu(acc[0:160, :] * inv) * (acc[160:320, :] * inv)).astype(BF)
    hidden = lax.dot_general(
        pick, hidden_t, (((1,), (1,)), ((), ())), preferred_element_type=F32
    ).astype(BF)
    share = jnp.sum(jnp.where(picked, row_share, 0.0), axis=1, keepdims=True)

    def product(core, n):
        b = 4 * (n // 2) + 2 * core + lax.rem(n, 2)
        k = pl.ds(pl.multiple_of(b * 1024, 1024), 1024)
        sums = (dot(hidden, cut[:, k]) * share).astype(BF)
        for j in range(8):
            partial[core, n // 2, j, lax.rem(n, 2)] = sums[:, j * 128 : j * 128 + 128]

    def other_half(n, _):
        product(1 - c, n)
        copy(
            partial.at[1 - c, n // 2, :, lax.rem(n, 2)], from_core.at[n // 2, :, lax.rem(n, 2)],
            c_send, c_recv, pool, sibling,
        ).start()
        return 0

    def own_half(n, _):
        product(c, n)
        return 0

    lax.fori_loop(0, 4, other_half, 0)
    lax.fori_loop(0, 4, own_half, 0)
    wait_bytes(from_core, c_recv)

    def chip_sum(spot_of):
        g, j = spot_of // 8, lax.rem(spot_of, 8)
        return (partial[c, g, j].astype(F32) + from_core[g, j].astype(F32)).astype(BF)

    def send_sum(d, _):
        to = lax.rem(spot + d, 16)
        to_group[to] = chip_sum(to)
        copy(
            to_group.at[to], from_group.at[spot], r_send, r_recv, pool, member(to, c)
        ).start()
        return 0

    lax.fori_loop(1, 16, send_sum, 0)
    from_group[spot] = chip_sum(spot)

    column = lax.dot_general(
        (r0 == r1).astype(BF), jnp.broadcast_to(own_places, (8, 256)).astype(BF),
        (((1,), (1,)), ((), ())), preferred_element_type=F32,
    )[:, 0:1]
    spread_by = (column == iota((256, SLOTS), 1).astype(F32)).astype(BF)
    wait_bytes(from_group.at[pl.ds(0, 15)], r_recv)

    for i in range(2):
        total = from_group[0, i].astype(F32)
        for s in range(1, 16):
            total += from_group[s, i].astype(F32)
        spread = dot(spread_by, total.astype(BF)).astype(BF)
        for p in range(2):
            to_rows[i, p] = spread[p * 128 : p * 128 + 128, :]
        for p in range(2):
            for core in range(2):
                r = rank_of(4 * zb + 2 * c + i, x, yh, core)
                src, dst = to_rows.at[i, p], from_experts.at[expert]
                here = is_self(p, r)

                @pl.when(here)
                def _():
                    pltpu.make_async_copy(src, dst, d_recv).start()

                @pl.when(jnp.logical_not(here))
                def _():
                    copy(src, dst, d_send, d_recv, p, r).start()

    wait_bytes(from_experts, d_recv)
    sums = from_experts[0].astype(F32)
    for e in range(1, 8):
        sums += from_experts[e].astype(F32)
    back = (iota((128, 56), 0) == iota((128, 56), 1) + 56 * c).astype(F32)
    mine_sum = jnp.dot(sums, back, preferred_element_type=F32, precision=lax.Precision.HIGHEST)
    out_ref[...] = (hstate.astype(F32) + mine_sum).astype(BF)

    wait_bytes(state_sent, m_send)

    @pl.when(across == 0)
    def _():
        wait_bytes(state_sent, m_send)

    wait_bytes(from_core, c_send)
    wait_bytes(from_group.at[pl.ds(0, 15)], r_send)
    wait_bytes(from_experts.at[pl.ds(0, 7)], d_send)

    @pl.when(jnp.logical_not(same))
    def _():
        wait_bytes(from_experts.at[0], d_send)


def local(
    queries, cache_keys, cache_values, new_keys, new_values, lengths, residual, out_weight,
    norm_gain, router_weight, routes, gate_tiles, up_tiles, down_tiles,
):
    dma = pltpu.SemaphoreType.DMA
    vmem = pltpu.VMEM
    gather_sems = [dma, dma((8,)), dma((2,)), dma((4, 2)), dma((4, 2)), dma, dma((8,))]
    return pl.pallas_call(
        layer_kernel,
        out_shape=jax.ShapeDtypeStruct((128, 56), BF),
        in_specs=[
            ANY, ANY, ANY, VM, VM, pl.BlockSpec(memory_space=pltpu.SMEM), ANY, ANY, VM, VM, VM,
            ANY, ANY, ANY,
        ],
        out_specs=VM,
        scratch_shapes=[
            vmem((64, 256), BF),
            vmem((2048, 256), BF),
            vmem((2048, 256), BF),
            vmem((128, 56), BF),
            vmem((56, 16384), BF),
            vmem((SLOTS, 7168), BF),
            vmem((SLOTS, 7168), BF),
            vmem((SLOTS, 7168), BF),
            vmem((336, 8192), BF),
            vmem((SLOTS, 8192), BF),
            vmem((8, 4, 2, 2, 128, 128), BF),
            vmem((8, 16, 16384), BF),
            vmem((2, 128, 128), BF),
            vmem((128, 128), BF),
            vmem((8, 4, 2, 2, 128, 128), BF),
            vmem((344, 256), F32),
            vmem((2, 2, 8, 2, SLOTS, 128), BF),
            vmem((2, 8, 2, SLOTS, 128), BF),
            vmem((16, 2, SLOTS, 128), BF),
            vmem((16, 2, SLOTS, 128), BF),
            vmem((2, 2, 128, 128), BF),
            vmem((8, 128, 128), BF),
            vmem((8, 256), F32),
            dma((8,)),
            *gather_sems,
            *gather_sems,
            dma, dma((2,)), dma, dma, dma, dma, dma, dma,
        ],
        compiler_params=pltpu.CompilerParams(
            collective_id=0, has_side_effects=True, vmem_limit_bytes=56 * 2**20
        ),
        name="decode_layer",
    )(
        queries, cache_keys, cache_values, new_keys, new_values, lengths, residual, out_weight,
        norm_gain.reshape(1, 7168), router_weight.T, routes.T, jnp.swapaxes(gate_tiles, 1, 2),
        jnp.swapaxes(up_tiles, 1, 2), down_tiles,
    )


def solution(mesh):
    return jax.shard_map(
        local,
        mesh=mesh,
        in_specs=(
            P(("pool", "rank"), None, None),
            P(("pool", "rank"), None, None),
            P(("pool", "rank"), None, None),
            P(("pool", "rank"), None),
            P(("pool", "rank"), None),
            P(("pool", "rank")),
            P("pool", "rank"),
            P("rank", None),
            P(),
            P(),
            P(),
            P(("pool", "rank"), None, None),
            P(("pool", "rank"), None, None),
            P(("pool", "rank"), None, None),
        ),
        out_specs=P("pool", "rank"),
        check_vma=False,
    )
```

```python
import jax
import jax.numpy as jnp
from jax import lax
from jax.experimental import pallas as pl
from jax.experimental.pallas import tpu as pltpu
from jax.sharding import PartitionSpec as P

MESH = pl.DeviceIdType.MESH
BF = jnp.bfloat16
F32 = jnp.float32
EPSILON = 1e-05
SLOTS = 160
WIDE = 112
VM = pl.BlockSpec(memory_space=pltpu.VMEM)
ANY = pl.BlockSpec(memory_space=pl.ANY)


def place(rank):
    return rank // 16, lax.rem(rank // 4, 4), lax.rem(rank // 2, 2), lax.rem(rank, 2)


def rank_of(z, x, yh, c):
    return z * 16 + x * 4 + yh * 2 + c


def iota(shape, dim):
    return lax.broadcasted_iota(jnp.int32, shape, dim)


def dot(a, b):
    return jnp.dot(a, b, preferred_element_type=F32)


def wait_bytes(ref, sem):
    pltpu.make_async_copy(ref, ref, sem).wait()


def padded(tiles):
    zeros = jnp.zeros((tiles[0].shape[0], 8), tiles[0].dtype)
    out = []
    for j in range(8):
        parts = []
        for start in (WIDE * j, WIDE * j + 56):
            while start % 56 or not parts or parts[-1] is zeros:
                end = min(start // 56 * 56 + 56, start // 128 * 128 + 128)
                base = start // 128 * 128
                parts.append(tiles[start // 128][:, start - base : end - base])
                start = end
                if start % 56 == 0:
                    break
            parts.append(zeros)
        out.append(jnp.concatenate(parts, axis=1))
    return out


def lane_tile(n):
    return pl.ds(pl.multiple_of(n * 128, 128), 128)


def layer_kernel(
    queries_hbm, keys_hbm, values_hbm, new_key_ref, new_value_ref, length_ref, residual_hbm,
    weight_hbm, gain_ref, router_ref, routes_ref, gate_hbm, up_hbm, down_hbm, out_ref,
    queries, keys, values, residual, weight, gate, up, down, fused, cut, rows_in, rows, states,
    acc, squares, partial, from_core, to_group, from_group, to_rows, from_experts,
    places, load_sem, a_plane, a_plane_in, a_ring, a_up_in, a_down_in, a_core, a_core_in, b_plane,
    b_plane_in, b_ring, b_up_in, b_down_in, b_core, b_core_in, c_send, c_recv,
    r_send, r_recv, d_send, d_recv,
):
    pool, rank = lax.axis_index("pool"), lax.axis_index("rank")
    z, x, yh, c = place(rank)
    zb = lax.rem(z, 2)
    expert = pool * 4 + z // 2
    spot = zb * 8 + x * 2 + yh
    sibling = rank + 1 - 2 * c
    up_rank = rank_of(lax.rem(z + 1, 8), x, yh, c)
    down_rank = rank_of(lax.rem(z + 7, 8), x, yh, c)
    same = jnp.logical_and(z // 4 == zb, lax.rem(z // 2, 2) == c)

    def member(spot_of, core):
        return (z // 2) * 32 + spot_of * 2 + core

    def copy(src, dst, send, recv, p, r):
        return pltpu.make_async_remote_copy(
            src_ref=src, dst_ref=dst, send_sem=send, recv_sem=recv, device_id=(p, r),
            device_id_type=MESH,
        )

    def in_plane(d):
        return lax.rem(pool + d // 8, 2), z * 16 + lax.rem(x * 2 + yh + d, 8) * 2 + c

    def is_self(p, r):
        return jnp.logical_and(p == pool, r == rank)

    loads = []
    for n, (src, dst) in enumerate((
        (queries_hbm.at[0], queries), (keys_hbm.at[0], keys), (values_hbm.at[0], values),
        (residual_hbm, residual), (weight_hbm, weight), (gate_hbm.at[0], gate),
        (up_hbm.at[0], up), (down_hbm.at[0], down),
    )):
        load = pltpu.make_async_copy(src, dst, load_sem.at[n])
        load.start()
        loads.append(load)

    barrier = pltpu.get_barrier_semaphore()

    def greet(p, r):
        @pl.when(jnp.logical_not(is_self(p, r)))
        def _():
            pl.semaphore_signal(barrier, inc=1, device_id=(p, r), device_id_type=MESH)

    def greet_plane(d, _):
        greet(*in_plane(d))
        return 0

    def greet_group(d, _):
        greet(pool, member((1 - zb) * 8 + d, c))
        return 0

    def greet_sums(e, _):
        greet(e // 4, rank_of(2 * lax.rem(e, 4) + z // 4, x, yh, lax.rem(z // 2, 2)))
        return 0

    lax.fori_loop(1, 16, greet_plane, 0)
    greet(pool, sibling)
    greet(pool, up_rank)
    greet(pool, down_rank)
    lax.fori_loop(0, 8, greet_group, 0)
    lax.fori_loop(0, 8, greet_sums, 0)

    loads[0].wait()
    loads[1].wait()
    q = queries[...]
    scores = lax.dot_general(
        q, keys[...], (((1,), (1,)), ((), ())), preferred_element_type=F32
    ) * (1.0 / 16.0)
    self_score = jnp.sum(
        q.astype(F32) * new_key_ref[...].astype(F32), axis=1, keepdims=True
    ) * (1.0 / 16.0)
    scores = jnp.where(iota((64, 2048), 1) < length_ref[0], scores, -1e30)
    highest = jnp.maximum(jnp.max(scores, axis=1, keepdims=True), self_score)
    raised = jnp.exp(scores - highest)
    raised_self = jnp.exp(self_score - highest)
    denominator = jnp.sum(raised, axis=1, keepdims=True) + raised_self
    weights = (raised / denominator).astype(BF)
    weight_self = (raised_self / denominator).astype(BF).astype(F32)
    loads[2].wait()
    context = dot(weights, values[...]) + weight_self * new_value_ref[...].astype(F32)
    context = context.astype(BF)
    rows_in[z, x, yh, c, 0:64, :] = context[:, 0:128]
    rows_in[z, x, yh, c, 64:128, :] = context[:, 128:256]

    pl.semaphore_wait(barrier, 34 - same.astype(jnp.int32))

    def gather(count, own, block, chunk, whole, plane, plane_in, ring, up_in, down_in, core_send, core_in, work):
        here = pool * 8 + x * 2 + yh

        def to_plane(d, _):
            p, r = in_plane(d)
            copy(own, own, plane, plane_in.at[here], p, r).start()
            return 0

        def landed(d, _):
            p, r = in_plane(d)
            _, rx, ry, _ = place(r)
            wait_bytes(block(p, rx, ry), plane_in.at[p * 8 + rx * 2 + ry])
            return 0

        lax.fori_loop(1, count, to_plane, 0)
        lax.fori_loop(1, count, landed, 0)

        def share(b, k):
            copy(chunk(b, k), chunk(b, k), core_send, core_in.at[b], pool, sibling).start()

        for s in range(5):
            b_up, b_down = lax.rem(z + 8 - s, 8), lax.rem(z + s, 8)
            for k in range(2):
                if s > 0 and (s < 4 or k == 0):
                    wait_bytes(chunk(b_up, k), up_in.at[s - 1, k])
                if s < 3 or (s == 3 and k == 0):
                    copy(chunk(b_up, k), chunk(b_up, k), ring.at[0], up_in.at[s, k], pool, up_rank).start()
                if s > 0 and (s < 4 or k == 1):
                    wait_bytes(chunk(b_down, k), down_in.at[s - 1, k])
                if s < 3 or (s == 3 and k == 1):
                    copy(chunk(b_down, k), chunk(b_down, k), ring.at[1], down_in.at[s, k], pool, down_rank).start()
                if s < 4 or k == 0:
                    share(b_up, k)
                if 0 < s < 4 or (s == 4 and k == 1):
                    share(b_down, k)
            work(s)

        def all_sent(d, _):
            wait_bytes(own, plane)
            return 0

        lax.fori_loop(1, count, all_sent, 0)
        for way in range(2):
            for n in range(7):
                wait_bytes(chunk(n, 0), ring.at[way])
        for n in range(8):
            wait_bytes(whole(n), core_send)

    def step_planes(s):
        if s in (0, 4):
            return [lax.rem(z + s, 8)]
        return [lax.rem(z + 8 - s, 8), lax.rem(z + s, 8)]

    def prepare(b, _):
        gains = padded([gain_ref[:, lane_tile(b * 7 + j)] for j in range(7)])
        routers = padded([router_ref[:, lane_tile(b * 7 + j)].astype(F32) for j in range(7)])
        for j in range(8):
            part = (routers[j] * gains[j]).astype(BF)
            fused[320:336, lane_tile(b * 8 + j)] = jnp.concatenate([part, jnp.zeros_like(part)], axis=0)

        def strip(n, _):
            r = pl.ds(pl.multiple_of(n * 32, 32), 32)
            for src, first in ((gate, 0), (up, SLOTS)):
                tiles = padded([src[r, lane_tile(b * 7 + j)] for j in range(7)])
                to = pl.ds(pl.multiple_of(first + n * 32, 32), 32)
                for j in range(8):
                    fused[to, lane_tile(b * 8 + j)] = (tiles[j].astype(F32) * gains[j]).astype(BF)
            tiles = padded([down[r, lane_tile(b * 7 + j)] for j in range(7)])
            for j in range(8):
                cut[r, lane_tile(b * 8 + j)] = tiles[j]
            return 0

        lax.fori_loop(0, 5, strip, 0)
        return 0

    def turn(b):
        def part(k, _):
            block = rows_in[b, :, :, :, pl.ds(pl.multiple_of(k * 16, 16), 16), :]
            block = jnp.swapaxes(block.reshape(16, 16, 128), 0, 1)
            for j in range(16):
                n = 2 * (lax.rem(k, 4) * 16 + j) + k // 4
                rows[b, :, lane_tile(n)] = block[j]
            return 0

        lax.fori_loop(0, 8, part, 0)

    def row_work(s):
        if s == 0:
            for load in loads[5:]:
                load.wait()
        if s < 4:
            lax.fori_loop(2 * s, 2 * s + 2, prepare, 0)
        for b in step_planes(s):
            wait_bytes(row_plane(b), a_core_in.at[b])
            turn(b)

    def row_plane(b):
        return rows_in.at[b, :, :, c]

    gather(
        8, rows_in.at[z, x, yh, c], lambda p, rx, ry: rows_in.at[z, rx, ry, c],
        lambda b, k: rows_in.at[b, pl.ds(2 * k, 2), :, c], row_plane, a_plane, a_plane_in, a_ring,
        a_up_in, a_down_in, a_core, a_core_in, row_work,
    )

    loads[3].wait()
    loads[4].wait()
    projected = lax.dot_general(
        weight[...], rows[...].reshape(128, 16384), (((1,), (1,)), ((), ())),
        preferred_element_type=F32,
    )
    hstate = (residual[...].astype(F32) + projected).astype(BF).astype(F32)
    states[z, pool, x, yh, c] = jnp.concatenate(
        [hstate, jnp.zeros((8, 128), F32)], axis=0
    ).astype(BF)

    rows8 = iota((8, 256), 0)
    members = jnp.zeros((8, 256), F32)
    for k in range(3):
        members += (routes_ref[k : k + 1, :] == rows8).astype(F32)
    r0, r1 = iota((256, 256), 0), iota((256, 256), 1)
    order = dot(members.astype(BF), (r0 < r1).astype(BF))
    places[...] = jnp.where(members > 0.5, order, -1.0)
    acc[...] = jnp.zeros_like(acc)
    squares[...] = jnp.zeros_like(squares)

    def state_work(s):
        for b in step_planes(s):
            wait_bytes(state_plane(b), b_core_in.at[b])
            k = pl.ds(pl.multiple_of(b * 1024, 1024), 1024)
            for p in range(2):
                part = states[b, p].reshape(1024, 128)
                lanes = slice(p * 128, p * 128 + 128)
                acc[:, lanes] += dot(fused[:, k], part)
                wide = part.astype(F32)
                squares[:, lanes] += jnp.sum((wide * wide).reshape(128, 8, 128), axis=0)

    def state_plane(b):
        return states.at[b, :, :, :, c]

    gather(
        16, states.at[z, pool, x, yh, c], lambda p, rx, ry: states.at[z, p, rx, ry, c],
        lambda b, k: states.at[b, k, :, :, c], state_plane, b_plane, b_plane_in, b_ring, b_up_in,
        b_down_in, b_core, b_core_in, state_work,
    )

    own_places = places[pl.ds(expert, 1), :]
    picked = own_places == iota((SLOTS, 256), 0).astype(F32)
    pick = picked.astype(BF)
    inv = lax.rsqrt(jnp.sum(squares[...], axis=0, keepdims=True) * (1.0 / 7168) + EPSILON)
    chosen = jax.nn.sigmoid(acc[320:328, :] * inv)
    named = jnp.where(members > 0.5, chosen, 0.0)
    whole = jnp.sum(named, axis=0, keepdims=True)
    row_share = jnp.sum(jnp.where(rows8 == expert, named, 0.0), axis=0, keepdims=True) / whole
    hidden_t = (jax.nn.silu(acc[0:160, :] * inv) * (acc[160:320, :] * inv)).astype(BF)
    hidden = lax.dot_general(
        pick, hidden_t, (((1,), (1,)), ((), ())), preferred_element_type=F32
    ).astype(BF)
    share = jnp.sum(jnp.where(picked, row_share, 0.0), axis=1, keepdims=True)

    def product(core, n):
        b = 4 * (n // 2) + 2 * core + lax.rem(n, 2)
        k = pl.ds(pl.multiple_of(b * 1024, 1024), 1024)
        sums = (dot(hidden, cut[:, k]) * share).astype(BF)
        for j in range(8):
            partial[core, n // 2, j, lax.rem(n, 2)] = sums[:, j * 128 : j * 128 + 128]

    def other_half(n, _):
        product(1 - c, n)
        copy(
            partial.at[1 - c, n // 2, :, lax.rem(n, 2)], from_core.at[n // 2, :, lax.rem(n, 2)],
            c_send, c_recv, pool, sibling,
        ).start()
        return 0

    def own_half(n, _):
        product(c, n)
        return 0

    lax.fori_loop(0, 4, other_half, 0)
    lax.fori_loop(0, 4, own_half, 0)
    wait_bytes(from_core, c_recv)

    def chip_sum(spot_of):
        g, j = spot_of // 8, lax.rem(spot_of, 8)
        return (partial[c, g, j].astype(F32) + from_core[g, j].astype(F32)).astype(BF)

    def send_sum(d, _):
        to = lax.rem(spot + d, 16)
        to_group[to] = chip_sum(to)
        copy(
            to_group.at[to], from_group.at[spot], r_send, r_recv, pool, member(to, c)
        ).start()
        return 0

    lax.fori_loop(1, 16, send_sum, 0)
    from_group[spot] = chip_sum(spot)
    wait_bytes(from_group.at[pl.ds(0, 15)], r_recv)

    for i in range(2):
        total = from_group[0, i].astype(F32)
        for s in range(1, 16):
            total += from_group[s, i].astype(F32)
        spread = lax.dot_general(
            total.astype(BF), pick, (((0,), (0,)), ((), ())), preferred_element_type=F32
        ).astype(BF)
        for p in range(2):
            for core in range(2):
                to_rows[i, p, core] = spread[core * 64 : core * 64 + 64, p * 128 : p * 128 + 128]
        for p in range(2):
            for core in range(2):
                r = rank_of(4 * zb + 2 * c + i, x, yh, core)
                src, dst = to_rows.at[i, p, core], from_experts.at[expert]
                here = is_self(p, r)

                @pl.when(here)
                def _():
                    pltpu.make_async_copy(src, dst, d_recv).start()

                @pl.when(jnp.logical_not(here))
                def _():
                    copy(src, dst, d_send, d_recv, p, r).start()

    wait_bytes(from_experts, d_recv)
    sums = from_experts[0].astype(F32)
    for e in range(1, 8):
        sums += from_experts[e].astype(F32)
    out_ref[...] = (hstate + sums[0:56]).astype(BF)

    wait_bytes(from_core, c_send)
    wait_bytes(from_group.at[pl.ds(0, 15)], r_send)
    wait_bytes(from_experts.at[pl.ds(0, 7)], d_send)

    @pl.when(jnp.logical_not(same))
    def _():
        wait_bytes(from_experts.at[0], d_send)


def local(
    queries, cache_keys, cache_values, new_keys, new_values, lengths, residual, out_weight,
    norm_gain, router_weight, routes, gate_tiles, up_tiles, down_tiles,
):
    dma = pltpu.SemaphoreType.DMA
    vmem = pltpu.VMEM
    gather_sems = [dma, dma((16,)), dma((2,)), dma((4, 2)), dma((4, 2)), dma, dma((8,))]
    return pl.pallas_call(
        layer_kernel,
        out_shape=jax.ShapeDtypeStruct((56, 128), BF),
        in_specs=[
            ANY, ANY, ANY, VM, VM, pl.BlockSpec(memory_space=pltpu.SMEM), ANY, ANY, VM, VM, VM,
            ANY, ANY, ANY,
        ],
        out_specs=VM,
        scratch_shapes=[
            vmem((64, 256), BF),
            vmem((2048, 256), BF),
            vmem((2048, 256), BF),
            vmem((56, 128), BF),
            vmem((56, 16384), BF),
            vmem((SLOTS, 7168), BF),
            vmem((SLOTS, 7168), BF),
            vmem((SLOTS, 7168), BF),
            vmem((336, 8192), BF),
            vmem((SLOTS, 8192), BF),
            vmem((8, 4, 2, 2, 128, 128), BF),
            vmem((8, 16, 16384), BF),
            vmem((8, 2, 4, 2, 2, 64, 128), BF),
            vmem((336, 256), F32),
            vmem((8, 256), F32),
            vmem((2, 2, 8, 2, SLOTS, 128), BF),
            vmem((2, 8, 2, SLOTS, 128), BF),
            vmem((16, 2, SLOTS, 128), BF),
            vmem((16, 2, SLOTS, 128), BF),
            vmem((2, 2, 2, 64, 128), BF),
            vmem((8, 64, 128), BF),
            vmem((8, 256), F32),
            dma((8,)),
            *gather_sems,
            *gather_sems,
            dma, dma, dma, dma, dma, dma,
        ],
        compiler_params=pltpu.CompilerParams(
            collective_id=0, has_side_effects=True, vmem_limit_bytes=56 * 2**20
        ),
        name="decode_layer",
    )(
        queries, cache_keys, cache_values, new_keys, new_values, lengths, residual.T, out_weight,
        norm_gain.reshape(1, 7168), router_weight.T, routes.T, jnp.swapaxes(gate_tiles, 1, 2),
        jnp.swapaxes(up_tiles, 1, 2), down_tiles,
    ).T


def solution(mesh):
    return jax.shard_map(
        local,
        mesh=mesh,
        in_specs=(
            P(("pool", "rank"), None, None),
            P(("pool", "rank"), None, None),
            P(("pool", "rank"), None, None),
            P(("pool", "rank"), None),
            P(("pool", "rank"), None),
            P(("pool", "rank")),
            P("pool", "rank"),
            P("rank", None),
            P(),
            P(),
            P(),
            P(("pool", "rank"), None, None),
            P(("pool", "rank"), None, None),
            P(("pool", "rank"), None, None),
        ),
        out_specs=P("pool", "rank"),
        check_vma=False,
    )
```

```python
import jax
import jax.numpy as jnp
from jax import lax
from jax.experimental import pallas as pl
from jax.experimental.pallas import tpu as pltpu
from jax.sharding import PartitionSpec as P

MESH = pl.DeviceIdType.MESH
BF = jnp.bfloat16
F32 = jnp.float32
EPSILON = 1e-05
SLOTS = 160
WIDE = 112
VM = pl.BlockSpec(memory_space=pltpu.VMEM)
ANY = pl.BlockSpec(memory_space=pl.ANY)


def place(rank):
    return rank // 16, lax.rem(rank // 4, 4), lax.rem(rank // 2, 2), lax.rem(rank, 2)


def rank_of(z, x, yh, c):
    return z * 16 + x * 4 + yh * 2 + c


def iota(shape, dim):
    return lax.broadcasted_iota(jnp.int32, shape, dim)


def dot(a, b):
    return jnp.dot(a, b, preferred_element_type=F32)


def wait_bytes(ref, sem):
    pltpu.make_async_copy(ref, ref, sem).wait()


def padded(tiles):
    zeros = jnp.zeros((tiles[0].shape[0], 8), tiles[0].dtype)
    out = []
    for j in range(8):
        parts = []
        for start in (WIDE * j, WIDE * j + 56):
            while start % 56 or not parts or parts[-1] is zeros:
                end = min(start // 56 * 56 + 56, start // 128 * 128 + 128)
                base = start // 128 * 128
                parts.append(tiles[start // 128][:, start - base : end - base])
                start = end
                if start % 56 == 0:
                    break
            parts.append(zeros)
        out.append(jnp.concatenate(parts, axis=1))
    return out


def lane_tile(n):
    return pl.ds(pl.multiple_of(n * 128, 128), 128)


def layer_kernel(
    queries_hbm, keys_hbm, values_hbm, new_key_ref, new_value_ref, length_ref, residual_hbm,
    weight_hbm, gain_ref, router_ref, routes_ref, gate_hbm, up_hbm, down_hbm, out_ref,
    queries, keys, values, residual, weight, gate, up, down, fused, cut, rows_in, rows, states,
    acc, squares, partial, from_core, to_group, from_group, to_rows, from_experts,
    places, load_sem, c_send, c_recv, r_send, r_recv, d_send, d_recv, *gather_sems,
):
    pool, rank = lax.axis_index("pool"), lax.axis_index("rank")
    z, x, yh, c = place(rank)
    zb = lax.rem(z, 2)
    expert = pool * 4 + z // 2
    spot = zb * 8 + x * 2 + yh
    sibling = rank + 1 - 2 * c
    same = jnp.logical_and(z // 4 == zb, lax.rem(z // 2, 2) == c)

    def member(spot_of, core):
        return (z // 2) * 32 + spot_of * 2 + core

    def copy(src, dst, send, recv, p, r):
        return pltpu.make_async_remote_copy(
            src_ref=src, dst_ref=dst, send_sem=send, recv_sem=recv, device_id=(p, r),
            device_id_type=MESH,
        )

    def in_plane(d, core):
        return lax.rem(pool + d // 8, 2), z * 16 + lax.rem(x * 2 + yh + d, 8) * 2 + core

    def is_self(p, r):
        return jnp.logical_and(p == pool, r == rank)

    loads = []
    for n, (src, dst) in enumerate((
        (queries_hbm.at[0], queries), (keys_hbm.at[0], keys), (values_hbm.at[0], values),
        (residual_hbm, residual), (weight_hbm, weight), (gate_hbm.at[0], gate),
        (up_hbm.at[0], up), (down_hbm.at[0], down),
    )):
        load = pltpu.make_async_copy(src, dst, load_sem.at[n])
        load.start()
        loads.append(load)

    barrier = pltpu.get_barrier_semaphore()

    def greet(p, r):
        @pl.when(jnp.logical_not(is_self(p, r)))
        def _():
            pl.semaphore_signal(barrier, inc=1, device_id=(p, r), device_id_type=MESH)

    def greet_plane(d, _):
        for core in range(2):
            greet(*in_plane(d, core))
        return 0

    def greet_line(d, _):
        for core in range(2):
            greet(pool, rank_of(lax.rem(z + d, 8), x, yh, core))
        return 0

    def greet_group(d, _):
        greet(pool, member((1 - zb) * 8 + d, c))
        return 0

    def greet_sums(e, _):
        greet(e // 4, rank_of(2 * lax.rem(e, 4) + z // 4, x, yh, lax.rem(z // 2, 2)))
        return 0

    greet(pool, sibling)

    @pl.when(c == 0)
    def _():
        lax.fori_loop(1, 16, greet_plane, 0)
        greet(pool, rank_of(lax.rem(z + 1, 8), x, yh, 0))
        greet(pool, rank_of(lax.rem(z + 7, 8), x, yh, 0))

    @pl.when(c == 1)
    def _():
        lax.fori_loop(1, 8, greet_line, 0)
        for n in (1, 3):
            greet(pool, rank_of(z, lax.rem(x + n, 4), yh, 1))
        greet(pool, rank_of(z, x, 1 - yh, 1))
        greet(1 - pool, rank)
        greet(1 - pool, rank_of(z, x, 1 - yh, 1))

        def greet_mates(d, _):
            greet(pool, z * 16 + lax.rem(x * 2 + yh + d, 8) * 2 + 1)
            return 0

        lax.fori_loop(1, 8, greet_mates, 0)

    lax.fori_loop(0, 8, greet_group, 0)
    lax.fori_loop(0, 8, greet_sums, 0)

    loads[0].wait()
    loads[1].wait()
    q = queries[...]
    scores = lax.dot_general(
        q, keys[...], (((1,), (1,)), ((), ())), preferred_element_type=F32
    ) * (1.0 / 16.0)
    self_score = jnp.sum(
        q.astype(F32) * new_key_ref[...].astype(F32), axis=1, keepdims=True
    ) * (1.0 / 16.0)
    scores = jnp.where(iota((64, 2048), 1) < length_ref[0], scores, -1e30)
    highest = jnp.maximum(jnp.max(scores, axis=1, keepdims=True), self_score)
    raised = jnp.exp(scores - highest)
    raised_self = jnp.exp(self_score - highest)
    denominator = jnp.sum(raised, axis=1, keepdims=True) + raised_self
    weights = (raised / denominator).astype(BF)
    weight_self = (raised_self / denominator).astype(BF).astype(F32)
    loads[2].wait()
    context = dot(weights, values[...]) + weight_self * new_value_ref[...].astype(F32)
    context = context.astype(BF)
    rows_in[z, x, yh, c, 0:64, :] = context[:, 0:128]
    rows_in[z, x, yh, c, 64:128, :] = context[:, 128:256]

    pl.semaphore_wait(barrier, 41 + 10 * c - same.astype(jnp.int32))

    def gather(buf, ny, w, device, sems, aside, work):
        (
            p_send, p_in, o_send, z_send, z_in, ring, up_in, down_in, y_send, y_in, x_send, l_in,
            r_in, ll_in, rr_in, s_send, s_in,
        ) = sems
        half = buf.shape[4] // 2
        first, second = pl.ds(0, half), pl.ds(half, half)
        flat = x * ny + w
        own = buf.at[z, x, w, c]

        def put(ref, send, recv, to):
            copy(ref, ref, send, recv, *to).start()

        def near(n, core):
            return device(lax.rem(z + n + 8, 8), x, w, core)

        def to_plane(d, _):
            f = lax.rem(flat + d, 4 * ny)
            put(own.at[first], p_send, p_in.at[flat * 2 + c], device(z, f // ny, lax.rem(f, ny), 0))
            return 0

        @pl.when(c == 1)
        def _():
            put(own.at[first], o_send, p_in.at[flat * 2 + 1], device(z, x, w, 0))

        @pl.when(c == 0)
        def _():
            put(own.at[second], o_send, z_in.at[z * 2], device(z, x, w, 1))

        put(own.at[second], z_send, z_in.at[z * 2 + c], near(1, 1))
        put(own.at[second], z_send, z_in.at[z * 2 + c], near(-1, 1))
        lax.fori_loop(1, 4 * ny, to_plane, 0)
        for n in (2, -2, 3, -3, 4):
            put(own.at[second], z_send, z_in.at[z * 2 + c], near(n, 1))

        def share(b, ref):
            put(ref, s_send, s_in.at[b], device(z, x, w, 1 - c))

        def share_near(core, rows):
            for i in range(1, ny):
                share(z, buf.at[z, x, lax.rem(w + i, ny), :, rows])
            share(z, buf.at[z, x, w, core, rows])

        def wait_plane(sem, rows, full):
            blocks = buf.reshape(64 * ny, 2 * half, 128)
            wait_bytes(blocks.at[pl.ds(0, 8 * ny if full else 8 * ny - 1), rows], sem)

        def finish(n, rows):
            for b in step_planes(n):
                wait_plane(s_in.at[b], rows, n > 0)
            work(step_planes(n))

        @pl.when(c == 0)
        def _():
            def chunk(b, q):
                return buf.at[b, lax.rem(x + (0, 1, 3, 2)[q], 4), :, :, first]

            aside(0, 0)
            for s in range(5):
                b_up, b_down = lax.rem(z + 8 - s, 8), lax.rem(z + s, 8)
                for q in range(4):
                    up_now, down_now = s < 4 or q < 2, s < 4 or q >= 2
                    if s == 0:
                        xx = lax.rem(x + (0, 1, 3, 2)[q], 4)
                        for i in range(ny):
                            ww = lax.rem(w + i, ny)
                            for core in range(2):
                                if q or i or core:
                                    wait_bytes(buf.at[z, xx, ww, core, first], p_in.at[(xx * ny + ww) * 2 + core])
                    if s > 0 and up_now:
                        wait_bytes(chunk(b_up, q), up_in.at[s - 1, q])
                    if s < 3 or (s == 3 and q < 2):
                        put(chunk(b_up, q), ring.at[0], up_in.at[s, q], near(1, 0))
                    if s > 0 and down_now:
                        wait_bytes(chunk(b_down, q), down_in.at[s - 1, q])
                    if s < 3 or (s == 3 and q >= 2):
                        put(chunk(b_down, q), ring.at[1], down_in.at[s, q], near(-1, 0))
                    if s == 0 and q == 0:
                        share_near(0, first)
                    elif s == 0 or up_now:
                        share(b_up, chunk(b_up, q))
                    if s > 0 and down_now:
                        share(b_down, chunk(b_down, q))
                if s < 4:
                    aside(0, s + 1)
            for n in range(5):
                finish(n, second)

            def ring_sent(n, _):
                for way in range(2):
                    wait_bytes(chunk(n, 0), ring.at[way])
                    wait_bytes(chunk(n, 0), ring.at[way])
                return 0

            lax.fori_loop(0, 7, ring_sent, 0)
            for n in range(8):
                wait_plane(s_send, first, n > 0)
            wait_bytes(own.at[second], o_send)

        @pl.when(c == 1)
        def _():
            left, right = device(z, lax.rem(x + 3, 4), w, 1), device(z, lax.rem(x + 1, 4), w, 1)
            lx, rx, ox = lax.rem(x + 3, 4), lax.rem(x + 1, 4), lax.rem(x + 2, 4)

            def along_z(n):
                for b in step_planes(n):
                    for core in range(2):
                        if n or core == 0:
                            wait_bytes(buf.at[b, x, w, core, second], z_in.at[b * 2 + core])
                    line = buf.at[b, x, w, :, second]
                    for i in range(1, ny):
                        put(line, y_send, y_in.at[b], device(z, x, lax.rem(w + i, ny), 1))

            def along_y(n):
                for b in step_planes(n):
                    wait_bytes(buf.at[b, x, pl.ds(0, ny - 1), :, second], y_in.at[b])
                    face = buf.at[b, x, :, :, second]
                    put(face, x_send, l_in.at[b], right)
                    put(face, x_send, r_in.at[b], left)
                    if n:
                        share(b, face)
                    else:
                        share_near(1, second)

            def along_x(n):
                for b in step_planes(n):
                    face = buf.at[b, lx, :, :, second]
                    wait_bytes(face, l_in.at[b])
                    put(buf.at[b, lx, pl.ds(0, ny // 2), :, second], x_send, ll_in.at[b], right)
                    share(b, face)
                    face = buf.at[b, rx, :, :, second]
                    wait_bytes(face, r_in.at[b])
                    put(buf.at[b, rx, pl.ds(ny // 2, ny // 2), :, second], x_send, rr_in.at[b], left)
                    share(b, face)

            def opposite(n):
                for b in step_planes(n):
                    wait_bytes(buf.at[b, ox, pl.ds(0, ny // 2), :, second], ll_in.at[b])
                    wait_bytes(buf.at[b, ox, pl.ds(ny // 2, ny // 2), :, second], rr_in.at[b])
                    share(b, buf.at[b, ox, :, :, second])

            aside(1, 0)
            along_z(0)
            along_z(1)
            along_y(0)
            for n in (2, 3, 4):
                along_z(n)
            aside(1, 1)
            along_y(1)
            along_y(2)
            aside(1, 2)
            along_y(3)
            along_y(4)
            along_x(0)
            along_x(1)
            aside(1, 3)
            for n in (2, 3, 4):
                along_x(n)
            for n in range(5):
                opposite(n)
            for n in range(5):
                finish(n, first)

            def line_sent(n, _):
                wait_bytes(buf.at[n, x, pl.ds(0, ny - 1), :, second], y_send)
                wait_bytes(buf.at[n, pl.ds(0, 3), :, :, second], x_send)
                return 0

            lax.fori_loop(0, 8, line_sent, 0)
            for n in range(8):
                wait_plane(s_send, second, n > 0)
            wait_bytes(own.at[first], o_send)

        def plane_sent(d, _):
            wait_bytes(own.at[first], p_send)
            return 0

        def line_sent(d, _):
            wait_bytes(own.at[second], z_send)
            return 0

        lax.fori_loop(1, 4 * ny, plane_sent, 0)
        lax.fori_loop(1, 8, line_sent, 0)

    def step_planes(s):
        if s in (0, 4):
            return [lax.rem(z + s, 8)]
        return [lax.rem(z + 8 - s, 8), lax.rem(z + s, 8)]

    def prepare(b, _):
        gains = padded([gain_ref[:, lane_tile(b * 7 + j)] for j in range(7)])
        routers = padded([router_ref[:, lane_tile(b * 7 + j)].astype(F32) for j in range(7)])
        for j in range(8):
            part = (routers[j] * gains[j]).astype(BF)
            fused[320:336, lane_tile(b * 8 + j)] = jnp.concatenate([part, jnp.zeros_like(part)], axis=0)

        def strip(n, _):
            r = pl.ds(pl.multiple_of(n * 32, 32), 32)
            for src, first in ((gate, 0), (up, SLOTS)):
                tiles = padded([src[r, lane_tile(b * 7 + j)] for j in range(7)])
                to = pl.ds(pl.multiple_of(first + n * 32, 32), 32)
                for j in range(8):
                    fused[to, lane_tile(b * 8 + j)] = (tiles[j].astype(F32) * gains[j]).astype(BF)
            tiles = padded([down[r, lane_tile(b * 7 + j)] for j in range(7)])
            for j in range(8):
                cut[r, lane_tile(b * 8 + j)] = tiles[j]
            return 0

        lax.fori_loop(0, 5, strip, 0)
        return 0

    def turn(b):
        def part(k, _):
            block = rows_in[b, :, :, :, pl.ds(pl.multiple_of(k * 16, 16), 16), :]
            block = jnp.swapaxes(block.reshape(16, 16, 128), 0, 1)
            for j in range(16):
                n = 2 * (lax.rem(k, 4) * 16 + j) + k // 4
                rows[b, :, lane_tile(n)] = block[j]
            return 0

        lax.fori_loop(0, 8, part, 0)

    def row_aside(core, n):
        if n == 0:
            for load in loads[5:]:
                load.wait()
        bounds = ((0, 2, 3, 5, 7, 8), (0, 3, 5, 7, 8))[core]
        lax.fori_loop(bounds[n], bounds[n + 1], prepare, 0)

    def row_work(planes):
        for b in planes:
            turn(b)

    def row_device(dz, dx, dw, core):
        return pool, rank_of(dz, dx, dw, core)

    gather(rows_in, 2, yh, row_device, gather_sems[:17], row_aside, row_work)

    loads[3].wait()
    loads[4].wait()
    projected = lax.dot_general(
        weight[...], rows[...].reshape(128, 16384), (((1,), (1,)), ((), ())),
        preferred_element_type=F32,
    )
    hstate = (residual[...].astype(F32) + projected).astype(BF).astype(F32)
    states[z, x, yh * 2 + pool, c] = jnp.concatenate(
        [hstate, jnp.zeros((8, 128), F32)], axis=0
    ).astype(BF)

    rows8 = iota((8, 256), 0)
    members = jnp.zeros((8, 256), F32)
    for k in range(3):
        members += (routes_ref[k : k + 1, :] == rows8).astype(F32)
    r0, r1 = iota((256, 256), 0), iota((256, 256), 1)
    order = dot(members.astype(BF), (r0 < r1).astype(BF))
    places[...] = jnp.where(members > 0.5, order, -1.0)
    acc[...] = jnp.zeros_like(acc)
    squares[...] = jnp.zeros_like(squares)

    def state_work(planes):
        for b in planes:
            k = pl.ds(pl.multiple_of(b * 1024, 1024), 1024)
            for p in range(2):
                part = jnp.concatenate(
                    [states[b, n // 2, (n % 2) * 2 + p].reshape(128, 128) for n in range(8)], axis=0
                )
                lanes = slice(p * 128, p * 128 + 128)
                acc[:, lanes] += dot(fused[:, k], part)
                wide = part.astype(F32)
                squares[:, lanes] += jnp.sum((wide * wide).reshape(128, 8, 128), axis=0)

    def state_device(dz, dx, dw, core):
        return lax.rem(dw, 2), rank_of(dz, dx, dw // 2, core)

    gather(
        states, 4, yh * 2 + pool, state_device, gather_sems[17:], lambda core, n: None, state_work
    )

    own_places = places[pl.ds(expert, 1), :]
    picked = own_places == iota((SLOTS, 256), 0).astype(F32)
    pick = picked.astype(BF)
    inv = lax.rsqrt(jnp.sum(squares[...], axis=0, keepdims=True) * (1.0 / 7168) + EPSILON)
    chosen = jax.nn.sigmoid(acc[320:328, :] * inv)
    named = jnp.where(members > 0.5, chosen, 0.0)
    whole = jnp.sum(named, axis=0, keepdims=True)
    row_share = jnp.sum(jnp.where(rows8 == expert, named, 0.0), axis=0, keepdims=True) / whole
    hidden_t = (jax.nn.silu(acc[0:160, :] * inv) * (acc[160:320, :] * inv)).astype(BF)
    hidden = lax.dot_general(
        pick, hidden_t, (((1,), (1,)), ((), ())), preferred_element_type=F32
    ).astype(BF)
    share = jnp.sum(jnp.where(picked, row_share, 0.0), axis=1, keepdims=True)

    def product(core, n):
        b = 4 * (n // 2) + 2 * core + lax.rem(n, 2)
        k = pl.ds(pl.multiple_of(b * 1024, 1024), 1024)
        sums = (dot(hidden, cut[:, k]) * share).astype(BF)
        for j in range(8):
            partial[core, n // 2, j, lax.rem(n, 2)] = sums[:, j * 128 : j * 128 + 128]

    def other_half(n, _):
        product(1 - c, n)
        copy(
            partial.at[1 - c, n // 2, :, lax.rem(n, 2)], from_core.at[n // 2, :, lax.rem(n, 2)],
            c_send, c_recv, pool, sibling,
        ).start()
        return 0

    def own_half(n, _):
        product(c, n)
        return 0

    lax.fori_loop(0, 4, other_half, 0)
    lax.fori_loop(0, 4, own_half, 0)
    wait_bytes(from_core, c_recv)

    def chip_sum(spot_of):
        g, j = spot_of // 8, lax.rem(spot_of, 8)
        return (partial[c, g, j].astype(F32) + from_core[g, j].astype(F32)).astype(BF)

    def send_sum(d, _):
        to = lax.rem(spot + d, 16)
        to_group[to] = chip_sum(to)
        copy(
            to_group.at[to], from_group.at[spot], r_send, r_recv, pool, member(to, c)
        ).start()
        return 0

    lax.fori_loop(1, 16, send_sum, 0)
    from_group[spot] = chip_sum(spot)
    wait_bytes(from_group.at[pl.ds(0, 15)], r_recv)

    for i in range(2):
        total = from_group[0, i].astype(F32)
        for s in range(1, 16):
            total += from_group[s, i].astype(F32)
        spread = lax.dot_general(
            total.astype(BF), pick, (((0,), (0,)), ((), ())), preferred_element_type=F32
        ).astype(BF)
        for p in range(2):
            for core in range(2):
                to_rows[i, p, core] = spread[core * 64 : core * 64 + 64, p * 128 : p * 128 + 128]
        for p in range(2):
            for core in range(2):
                r = rank_of(4 * zb + 2 * c + i, x, yh, core)
                src, dst = to_rows.at[i, p, core], from_experts.at[expert]
                here = is_self(p, r)

                @pl.when(here)
                def _():
                    pltpu.make_async_copy(src, dst, d_recv).start()

                @pl.when(jnp.logical_not(here))
                def _():
                    copy(src, dst, d_send, d_recv, p, r).start()

    wait_bytes(from_experts, d_recv)
    sums = from_experts[0].astype(F32)
    for e in range(1, 8):
        sums += from_experts[e].astype(F32)
    out_ref[...] = (hstate + sums[0:56]).astype(BF)

    wait_bytes(from_core, c_send)
    wait_bytes(from_group.at[pl.ds(0, 15)], r_send)
    wait_bytes(from_experts.at[pl.ds(0, 7)], d_send)

    @pl.when(jnp.logical_not(same))
    def _():
        wait_bytes(from_experts.at[0], d_send)


def local(
    queries, cache_keys, cache_values, new_keys, new_values, lengths, residual, out_weight,
    norm_gain, router_weight, routes, gate_tiles, up_tiles, down_tiles,
):
    dma = pltpu.SemaphoreType.DMA
    vmem = pltpu.VMEM

    def gather_sems(ny):
        return [
            dma, dma((8 * ny,)), dma, dma, dma((16,)), dma((2,)), dma((4, 4)), dma((4, 4)), dma,
            dma((8,)), dma, dma((8,)), dma((8,)), dma((8,)), dma((8,)), dma, dma((8,)),
        ]

    return pl.pallas_call(
        layer_kernel,
        out_shape=jax.ShapeDtypeStruct((56, 128), BF),
        in_specs=[
            ANY, ANY, ANY, VM, VM, pl.BlockSpec(memory_space=pltpu.SMEM), ANY, ANY, VM, VM, VM,
            ANY, ANY, ANY,
        ],
        out_specs=VM,
        scratch_shapes=[
            vmem((64, 256), BF),
            vmem((2048, 256), BF),
            vmem((2048, 256), BF),
            vmem((56, 128), BF),
            vmem((56, 16384), BF),
            vmem((SLOTS, 7168), BF),
            vmem((SLOTS, 7168), BF),
            vmem((SLOTS, 7168), BF),
            vmem((336, 8192), BF),
            vmem((SLOTS, 8192), BF),
            vmem((8, 4, 2, 2, 128, 128), BF),
            vmem((8, 16, 16384), BF),
            vmem((8, 4, 4, 2, 64, 128), BF),
            vmem((336, 256), F32),
            vmem((8, 256), F32),
            vmem((2, 2, 8, 2, SLOTS, 128), BF),
            vmem((2, 8, 2, SLOTS, 128), BF),
            vmem((16, 2, SLOTS, 128), BF),
            vmem((16, 2, SLOTS, 128), BF),
            vmem((2, 2, 2, 64, 128), BF),
            vmem((8, 64, 128), BF),
            vmem((8, 256), F32),
            dma((8,)),
            dma, dma, dma, dma, dma, dma,
            *gather_sems(2),
            *gather_sems(4),
        ],
        compiler_params=pltpu.CompilerParams(
            collective_id=0, has_side_effects=True, vmem_limit_bytes=56 * 2**20
        ),
        name="decode_layer",
    )(
        queries, cache_keys, cache_values, new_keys, new_values, lengths, residual.T, out_weight,
        norm_gain.reshape(1, 7168), router_weight.T, routes.T, jnp.swapaxes(gate_tiles, 1, 2),
        jnp.swapaxes(up_tiles, 1, 2), down_tiles,
    ).T


def solution(mesh):
    return jax.shard_map(
        local,
        mesh=mesh,
        in_specs=(
            P(("pool", "rank"), None, None),
            P(("pool", "rank"), None, None),
            P(("pool", "rank"), None, None),
            P(("pool", "rank"), None),
            P(("pool", "rank"), None),
            P(("pool", "rank")),
            P("pool", "rank"),
            P("rank", None),
            P(),
            P(),
            P(),
            P(("pool", "rank"), None, None),
            P(("pool", "rank"), None, None),
            P(("pool", "rank"), None, None),
        ),
        out_specs=P("pool", "rank"),
        check_vma=False,
    )
```

```python
import jax
import jax.numpy as jnp
from jax import lax
from jax.experimental import pallas as pl
from jax.experimental.pallas import tpu as pltpu
from jax.sharding import PartitionSpec as P

MESH = pl.DeviceIdType.MESH
BF = jnp.bfloat16
F32 = jnp.float32
EPSILON = 1e-05
SLOTS = 160
WIDE = 112
VM = pl.BlockSpec(memory_space=pltpu.VMEM)
ANY = pl.BlockSpec(memory_space=pl.ANY)


def place(rank):
    return rank // 16, lax.rem(rank // 4, 4), lax.rem(rank // 2, 2), lax.rem(rank, 2)


def rank_of(z, x, yh, c):
    return z * 16 + x * 4 + yh * 2 + c


def iota(shape, dim):
    return lax.broadcasted_iota(jnp.int32, shape, dim)


def dot(a, b):
    return jnp.dot(a, b, preferred_element_type=F32)


def wait_bytes(ref, sem):
    pltpu.make_async_copy(ref, ref, sem).wait()


def padded(tiles):
    zeros = jnp.zeros((tiles[0].shape[0], 8), tiles[0].dtype)
    out = []
    for j in range(8):
        parts = []
        for start in (WIDE * j, WIDE * j + 56):
            while start % 56 or not parts or parts[-1] is zeros:
                end = min(start // 56 * 56 + 56, start // 128 * 128 + 128)
                base = start // 128 * 128
                parts.append(tiles[start // 128][:, start - base : end - base])
                start = end
                if start % 56 == 0:
                    break
            parts.append(zeros)
        out.append(jnp.concatenate(parts, axis=1))
    return out


def lane_tile(n):
    return pl.ds(pl.multiple_of(n * 128, 128), 128)


def layer_kernel(
    queries_hbm, keys_hbm, values_hbm, new_key_hbm, new_value_hbm, length_hbm, residual_hbm,
    weight_hbm, gain_hbm, router_hbm, routes_hbm, gate_hbm, up_hbm, down_hbm, out_ref,
    new_key_ref, new_value_ref, length_ref, gain_ref, router_ref, routes_ref, queries, keys, values, residual, weight, gate, up, down, fused, cut, rows_in, rows, states,
    acc, squares, partial, from_core, to_group, from_group, to_rows, from_experts,
    places, load_sem, c_send, c_recv, r_send, r_recv, d_send, d_recv, *gather_sems,
):
    pool, rank = lax.axis_index("pool"), lax.axis_index("rank")
    z, x, yh, c = place(rank)
    zb = lax.rem(z, 2)
    expert = pool * 4 + z // 2
    spot = zb * 8 + x * 2 + yh
    sibling = rank + 1 - 2 * c
    same = jnp.logical_and(z // 4 == zb, lax.rem(z // 2, 2) == c)

    def member(spot_of, core):
        return (z // 2) * 32 + spot_of * 2 + core

    def copy(src, dst, send, recv, p, r):
        return pltpu.make_async_remote_copy(
            src_ref=src, dst_ref=dst, send_sem=send, recv_sem=recv, device_id=(p, r),
            device_id_type=MESH,
        )

    def in_plane(d, core):
        return lax.rem(pool + d // 8, 2), z * 16 + lax.rem(x * 2 + yh + d, 8) * 2 + core

    def is_self(p, r):
        return jnp.logical_and(p == pool, r == rank)

    loads = {}
    for n, (name, src, dst) in enumerate((
        ("queries", queries_hbm.at[0], queries), ("keys", keys_hbm.at[0], keys),
        ("new_key", new_key_hbm, new_key_ref), ("length", length_hbm, length_ref),
        ("values", values_hbm.at[0], values), ("new_value", new_value_hbm, new_value_ref),
        ("gain", gain_hbm, gain_ref), ("router", router_hbm, router_ref),
        ("gate", gate_hbm.at[0], gate), ("up", up_hbm.at[0], up), ("down", down_hbm.at[0], down),
        ("weight", weight_hbm, weight), ("residual", residual_hbm, residual),
        ("routes", routes_hbm, routes_ref),
    )):
        loads[name] = pltpu.make_async_copy(src, dst, load_sem.at[n])
        loads[name].start()

    def loaded(*names):
        for name in names:
            loads[name].wait()

    barrier = pltpu.get_barrier_semaphore()

    def greet(p, r):
        @pl.when(jnp.logical_not(is_self(p, r)))
        def _():
            pl.semaphore_signal(barrier, inc=1, device_id=(p, r), device_id_type=MESH)

    def greet_plane(d, _):
        for core in range(2):
            greet(*in_plane(d, core))
        return 0

    def greet_line(d, _):
        for core in range(2):
            greet(pool, rank_of(lax.rem(z + d, 8), x, yh, core))
        return 0

    greet(pool, sibling)

    @pl.when(c == 0)
    def _():
        lax.fori_loop(1, 16, greet_plane, 0)
        greet(pool, rank_of(lax.rem(z + 1, 8), x, yh, 0))
        greet(pool, rank_of(lax.rem(z + 7, 8), x, yh, 0))

    @pl.when(c == 1)
    def _():
        lax.fori_loop(1, 8, greet_line, 0)
        for n in (1, 3):
            greet(pool, rank_of(z, lax.rem(x + n, 4), yh, 1))
        greet(pool, rank_of(z, x, 1 - yh, 1))
        greet(1 - pool, rank)
        greet(1 - pool, rank_of(z, x, 1 - yh, 1))

    loaded("queries", "keys", "new_key", "length")
    q = queries[...]
    scores = lax.dot_general(
        q, keys[...], (((1,), (1,)), ((), ())), preferred_element_type=F32
    ) * (1.0 / 16.0)
    self_score = jnp.sum(
        q.astype(F32) * new_key_ref[...].astype(F32), axis=1, keepdims=True
    ) * (1.0 / 16.0)
    scores = jnp.where(iota((64, 2048), 1) < length_ref[...], scores, -1e30)
    highest = jnp.maximum(jnp.max(scores, axis=1, keepdims=True), self_score)
    raised = jnp.exp(scores - highest)
    raised_self = jnp.exp(self_score - highest)
    denominator = jnp.sum(raised, axis=1, keepdims=True) + raised_self
    weights = (raised / denominator).astype(BF)
    weight_self = (raised_self / denominator).astype(BF).astype(F32)
    loaded("values", "new_value")
    context = dot(weights, values[...]) + weight_self * new_value_ref[...].astype(F32)
    context = context.astype(BF)
    rows_in[z, x, yh, c, 0:64, :] = context[:, 0:128]
    rows_in[z, x, yh, c, 64:128, :] = context[:, 128:256]

    pl.semaphore_wait(barrier, 25 + 3 * c)

    def gather(buf, ny, w, device, sems, aside, work):
        (
            p_send, p_in, o_send, z_send, z_in, ring, up_in, down_in, y_send, y_in, x_send, l_in,
            r_in, ll_in, rr_in, s_send, s_in,
        ) = sems
        half = buf.shape[4] // 2
        first, second = pl.ds(0, half), pl.ds(half, half)
        flat = x * ny + w
        own = buf.at[z, x, w, c]

        def put(ref, send, recv, to):
            copy(ref, ref, send, recv, *to).start()

        def near(n, core):
            return device(lax.rem(z + n + 8, 8), x, w, core)

        def to_plane(d, _):
            f = lax.rem(flat + d, 4 * ny)
            put(own.at[first], p_send, p_in.at[flat * 2 + c], device(z, f // ny, lax.rem(f, ny), 0))
            return 0

        @pl.when(c == 1)
        def _():
            put(own.at[first], o_send, p_in.at[flat * 2 + 1], device(z, x, w, 0))

        @pl.when(c == 0)
        def _():
            put(own.at[second], o_send, z_in.at[z * 2], device(z, x, w, 1))

        put(own.at[second], z_send, z_in.at[z * 2 + c], near(1, 1))
        put(own.at[second], z_send, z_in.at[z * 2 + c], near(-1, 1))
        lax.fori_loop(1, 4 * ny, to_plane, 0)
        for n in (2, -2, 3, -3, 4):
            put(own.at[second], z_send, z_in.at[z * 2 + c], near(n, 1))

        def share(b, ref):
            put(ref, s_send, s_in.at[b], device(z, x, w, 1 - c))

        def share_near(core, rows):
            for i in range(1, ny):
                share(z, buf.at[z, x, lax.rem(w + i, ny), :, rows])
            share(z, buf.at[z, x, w, core, rows])

        def wait_plane(sem, rows, full):
            blocks = buf.reshape(64 * ny, 2 * half, 128)
            wait_bytes(blocks.at[pl.ds(0, 8 * ny if full else 8 * ny - 1), rows], sem)

        def finish(n, rows):
            for b in step_planes(n):
                wait_plane(s_in.at[b], rows, n > 0)
            work(step_planes(n))

        @pl.when(c == 0)
        def _():
            def chunk(b, q):
                return buf.at[b, lax.rem(x + (0, 1, 3, 2)[q], 4), :, :, first]

            aside(0, 0)
            for s in range(5):
                b_up, b_down = lax.rem(z + 8 - s, 8), lax.rem(z + s, 8)
                for q in range(4):
                    up_now, down_now = s < 4 or q < 2, s < 4 or q >= 2
                    if s == 0:
                        xx = lax.rem(x + (0, 1, 3, 2)[q], 4)
                        for i in range(ny):
                            ww = lax.rem(w + i, ny)
                            for core in range(2):
                                if q or i or core:
                                    wait_bytes(buf.at[z, xx, ww, core, first], p_in.at[(xx * ny + ww) * 2 + core])
                    if s > 0 and up_now:
                        wait_bytes(chunk(b_up, q), up_in.at[s - 1, q])
                    if s < 3 or (s == 3 and q < 2):
                        put(chunk(b_up, q), ring.at[0], up_in.at[s, q], near(1, 0))
                    if s > 0 and down_now:
                        wait_bytes(chunk(b_down, q), down_in.at[s - 1, q])
                    if s < 3 or (s == 3 and q >= 2):
                        put(chunk(b_down, q), ring.at[1], down_in.at[s, q], near(-1, 0))
                    if s == 0 and q == 0:
                        share_near(0, first)
                    elif s == 0 or up_now:
                        share(b_up, chunk(b_up, q))
                    if s > 0 and down_now:
                        share(b_down, chunk(b_down, q))
                if s < 4:
                    aside(0, s + 1)
            for n in range(5):
                finish(n, second)

            def ring_sent(n, _):
                for way in range(2):
                    wait_bytes(chunk(n, 0), ring.at[way])
                    wait_bytes(chunk(n, 0), ring.at[way])
                return 0

            lax.fori_loop(0, 7, ring_sent, 0)
            for n in range(8):
                wait_plane(s_send, first, n > 0)
            wait_bytes(own.at[second], o_send)

        @pl.when(c == 1)
        def _():
            left, right = device(z, lax.rem(x + 3, 4), w, 1), device(z, lax.rem(x + 1, 4), w, 1)
            lx, rx, ox = lax.rem(x + 3, 4), lax.rem(x + 1, 4), lax.rem(x + 2, 4)

            def along_z(n):
                for b in step_planes(n):
                    for core in range(2):
                        if n or core == 0:
                            wait_bytes(buf.at[b, x, w, core, second], z_in.at[b * 2 + core])
                    line = buf.at[b, x, w, :, second]
                    for i in range(1, ny):
                        put(line, y_send, y_in.at[b], device(z, x, lax.rem(w + i, ny), 1))

            def along_y(n):
                for b in step_planes(n):
                    wait_bytes(buf.at[b, x, pl.ds(0, ny - 1), :, second], y_in.at[b])
                    face = buf.at[b, x, :, :, second]
                    put(face, x_send, l_in.at[b], right)
                    put(face, x_send, r_in.at[b], left)
                    if n:
                        share(b, face)
                    else:
                        share_near(1, second)

            def along_x(n):
                for b in step_planes(n):
                    face = buf.at[b, lx, :, :, second]
                    wait_bytes(face, l_in.at[b])
                    put(buf.at[b, lx, pl.ds(0, ny // 2), :, second], x_send, ll_in.at[b], right)
                    share(b, face)
                    face = buf.at[b, rx, :, :, second]
                    wait_bytes(face, r_in.at[b])
                    put(buf.at[b, rx, pl.ds(ny // 2, ny // 2), :, second], x_send, rr_in.at[b], left)
                    share(b, face)

            def opposite(n):
                for b in step_planes(n):
                    wait_bytes(buf.at[b, ox, pl.ds(0, ny // 2), :, second], ll_in.at[b])
                    wait_bytes(buf.at[b, ox, pl.ds(ny // 2, ny // 2), :, second], rr_in.at[b])
                    share(b, buf.at[b, ox, :, :, second])

            aside(1, 0)
            along_z(0)
            along_z(1)
            along_y(0)
            for n in (2, 3, 4):
                along_z(n)
            aside(1, 1)
            along_y(1)
            along_y(2)
            aside(1, 2)
            along_y(3)
            along_y(4)
            along_x(0)
            along_x(1)
            aside(1, 3)
            for n in (2, 3, 4):
                along_x(n)
            for n in range(5):
                opposite(n)
            for n in range(5):
                finish(n, first)

            def line_sent(n, _):
                wait_bytes(buf.at[n, x, pl.ds(0, ny - 1), :, second], y_send)
                wait_bytes(buf.at[n, pl.ds(0, 3), :, :, second], x_send)
                return 0

            lax.fori_loop(0, 8, line_sent, 0)
            for n in range(8):
                wait_plane(s_send, second, n > 0)
            wait_bytes(own.at[first], o_send)

        def plane_sent(d, _):
            wait_bytes(own.at[first], p_send)
            return 0

        def line_sent(d, _):
            wait_bytes(own.at[second], z_send)
            return 0

        lax.fori_loop(1, 4 * ny, plane_sent, 0)
        lax.fori_loop(1, 8, line_sent, 0)

    def step_planes(s):
        if s in (0, 4):
            return [lax.rem(z + s, 8)]
        return [lax.rem(z + 8 - s, 8), lax.rem(z + s, 8)]

    def prepare(b, _):
        gains = padded([gain_ref[:, lane_tile(b * 7 + j)] for j in range(7)])
        routers = padded([router_ref[:, lane_tile(b * 7 + j)].astype(F32) for j in range(7)])
        for j in range(8):
            part = (routers[j] * gains[j]).astype(BF)
            fused[320:336, lane_tile(b * 8 + j)] = jnp.concatenate([part, jnp.zeros_like(part)], axis=0)

        def strip(n, _):
            r = pl.ds(pl.multiple_of(n * 32, 32), 32)
            for src, first in ((gate, 0), (up, SLOTS)):
                tiles = padded([src[r, lane_tile(b * 7 + j)] for j in range(7)])
                to = pl.ds(pl.multiple_of(first + n * 32, 32), 32)
                for j in range(8):
                    fused[to, lane_tile(b * 8 + j)] = (tiles[j].astype(F32) * gains[j]).astype(BF)
            tiles = padded([down[r, lane_tile(b * 7 + j)] for j in range(7)])
            for j in range(8):
                cut[r, lane_tile(b * 8 + j)] = tiles[j]
            return 0

        lax.fori_loop(0, 5, strip, 0)
        return 0

    def turn(b):
        def part(k, _):
            block = rows_in[b, :, :, :, pl.ds(pl.multiple_of(k * 16, 16), 16), :]
            block = jnp.swapaxes(block.reshape(16, 16, 128), 0, 1)
            for j in range(16):
                n = 2 * (lax.rem(k, 4) * 16 + j) + k // 4
                rows[b, :, lane_tile(n)] = block[j]
            return 0

        lax.fori_loop(0, 8, part, 0)

    def row_aside(core, n):
        if n == 0:
            loaded("gain", "router", "gate", "up", "down")
        bounds = ((0, 2, 3, 5, 7, 8), (0, 3, 5, 7, 8))[core]
        lax.fori_loop(bounds[n], bounds[n + 1], prepare, 0)

    def row_work(planes):
        for b in planes:
            turn(b)

    def row_device(dz, dx, dw, core):
        return pool, rank_of(dz, dx, dw, core)

    gather(rows_in, 2, yh, row_device, gather_sems[:17], row_aside, row_work)

    loaded("weight", "residual", "routes")
    projected = lax.dot_general(
        weight[...], rows[...].reshape(128, 16384), (((1,), (1,)), ((), ())),
        preferred_element_type=F32,
    )
    hstate = (residual[...].astype(F32) + projected).astype(BF).astype(F32)
    states[z, x, yh * 2 + pool, c] = jnp.concatenate(
        [hstate, jnp.zeros((8, 128), F32)], axis=0
    ).astype(BF)

    rows8 = iota((8, 256), 0)
    members = jnp.zeros((8, 256), F32)
    for k in range(3):
        members += (routes_ref[k : k + 1, :] == rows8).astype(F32)
    r0, r1 = iota((256, 256), 0), iota((256, 256), 1)
    order = dot(members.astype(BF), (r0 < r1).astype(BF))
    places[...] = jnp.where(members > 0.5, order, -1.0)
    acc[...] = jnp.zeros_like(acc)
    squares[...] = jnp.zeros_like(squares)

    def state_work(planes):
        for b in planes:
            k = pl.ds(pl.multiple_of(b * 1024, 1024), 1024)
            for p in range(2):
                part = jnp.concatenate(
                    [states[b, n // 2, (n % 2) * 2 + p].reshape(128, 128) for n in range(8)], axis=0
                )
                lanes = slice(p * 128, p * 128 + 128)
                acc[:, lanes] += dot(fused[:, k], part)
                wide = part.astype(F32)
                squares[:, lanes] += jnp.sum((wide * wide).reshape(128, 8, 128), axis=0)

    def state_device(dz, dx, dw, core):
        return lax.rem(dw, 2), rank_of(dz, dx, dw // 2, core)

    gather(
        states, 4, yh * 2 + pool, state_device, gather_sems[17:], lambda core, n: None, state_work
    )

    own_places = places[pl.ds(expert, 1), :]
    picked = own_places == iota((SLOTS, 256), 0).astype(F32)
    pick = picked.astype(BF)
    inv = lax.rsqrt(jnp.sum(squares[...], axis=0, keepdims=True) * (1.0 / 7168) + EPSILON)
    chosen = jax.nn.sigmoid(acc[320:328, :] * inv)
    named = jnp.where(members > 0.5, chosen, 0.0)
    whole = jnp.sum(named, axis=0, keepdims=True)
    row_share = jnp.sum(jnp.where(rows8 == expert, named, 0.0), axis=0, keepdims=True) / whole
    hidden_t = (jax.nn.silu(acc[0:160, :] * inv) * (acc[160:320, :] * inv)).astype(BF)
    hidden = lax.dot_general(
        pick, hidden_t, (((1,), (1,)), ((), ())), preferred_element_type=F32
    ).astype(BF)
    share = jnp.sum(jnp.where(picked, row_share, 0.0), axis=1, keepdims=True)

    def product(core, g, i):
        b = 4 * g + 2 * core + i
        k = pl.ds(pl.multiple_of(b * 1024, 1024), 1024)
        sums = (dot(hidden, cut[:, k]) * share).astype(BF)
        for j in range(8):
            partial[core, i, g, j] = sums[:, j * 128 : j * 128 + 128]

    def for_other(g, i):
        product(1 - c, g, i)
        copy(
            partial.at[1 - c, i, g], from_core.at[i, g], c_send, c_recv.at[2 * i + g], pool, sibling
        ).start()

    def send_sums(g, i):
        wait_bytes(from_core.at[i, g], c_recv.at[2 * i + g])

        def one(j, _):
            to = g * 8 + j
            both = (partial[c, i, g, j].astype(F32) + from_core[i, g, j].astype(F32)).astype(BF)

            @pl.when(to == spot)
            def _():
                from_group[i, to] = both

            @pl.when(to != spot)
            def _():
                to_group[i, to] = both
                copy(
                    to_group.at[i, to], from_group.at[i, spot], r_send, r_recv.at[i], pool,
                    member(to, c),
                ).start()

            return 0

        lax.fori_loop(0, 8, one, 0)

    parts = ((0, 0), (1, 0), (0, 1), (1, 1))
    for_other(*parts[0])
    for_other(*parts[1])
    product(c, *parts[0])
    for n in range(4):
        if n < 2:
            for_other(*parts[n + 2])
        if n < 3:
            product(c, *parts[n + 1])
        send_sums(*parts[n])

    for i in range(2):
        wait_bytes(from_group.at[i, pl.ds(0, 15)], r_recv.at[i])
        total = from_group[i, 0].astype(F32)
        for s in range(1, 16):
            total += from_group[i, s].astype(F32)
        spread = lax.dot_general(
            total.astype(BF), pick, (((0,), (0,)), ((), ())), preferred_element_type=F32
        ).astype(BF)
        for p in range(2):
            for core in range(2):
                to_rows[i, p, core] = spread[core * 64 : core * 64 + 64, p * 128 : p * 128 + 128]
        for p in range(2):
            for core in range(2):
                r = rank_of(4 * zb + 2 * c + i, x, yh, core)
                src, dst = to_rows.at[i, p, core], from_experts.at[expert]
                here = is_self(p, r)

                @pl.when(here)
                def _():
                    pltpu.make_async_copy(src, dst, d_recv).start()

                @pl.when(jnp.logical_not(here))
                def _():
                    copy(src, dst, d_send, d_recv, p, r).start()

    wait_bytes(from_experts, d_recv)
    sums = from_experts[0].astype(F32)
    for e in range(1, 8):
        sums += from_experts[e].astype(F32)
    out_ref[...] = (hstate + sums[0:56]).astype(BF)

    wait_bytes(from_core, c_send)
    wait_bytes(from_group.at[:, pl.ds(0, 15)], r_send)
    wait_bytes(from_experts.at[pl.ds(0, 7)], d_send)

    @pl.when(jnp.logical_not(same))
    def _():
        wait_bytes(from_experts.at[0], d_send)


def local(
    queries, cache_keys, cache_values, new_keys, new_values, lengths, residual, out_weight,
    norm_gain, router_weight, routes, gate_tiles, up_tiles, down_tiles,
):
    dma = pltpu.SemaphoreType.DMA
    vmem = pltpu.VMEM

    def gather_sems(ny):
        return [
            dma, dma((8 * ny,)), dma, dma, dma((16,)), dma((2,)), dma((4, 4)), dma((4, 4)), dma,
            dma((8,)), dma, dma((8,)), dma((8,)), dma((8,)), dma((8,)), dma, dma((8,)),
        ]

    return pl.pallas_call(
        layer_kernel,
        out_shape=jax.ShapeDtypeStruct((56, 128), BF),
        in_specs=[
            ANY, ANY, ANY, ANY, ANY, ANY, ANY, ANY, ANY, ANY, ANY, ANY, ANY, ANY,
        ],
        out_specs=VM,
        scratch_shapes=[
            vmem((1, 256), BF),
            vmem((1, 256), BF),
            vmem((1, 1), jnp.int32),
            vmem((1, 7168), F32),
            vmem((8, 7168), BF),
            vmem((3, 256), jnp.int32),
            vmem((64, 256), BF),
            vmem((2048, 256), BF),
            vmem((2048, 256), BF),
            vmem((56, 128), BF),
            vmem((56, 16384), BF),
            vmem((SLOTS, 7168), BF),
            vmem((SLOTS, 7168), BF),
            vmem((SLOTS, 7168), BF),
            vmem((336, 8192), BF),
            vmem((SLOTS, 8192), BF),
            vmem((8, 4, 2, 2, 128, 128), BF),
            vmem((8, 16, 16384), BF),
            vmem((8, 4, 4, 2, 64, 128), BF),
            vmem((336, 256), F32),
            vmem((8, 256), F32),
            vmem((2, 2, 2, 8, SLOTS, 128), BF),
            vmem((2, 2, 8, SLOTS, 128), BF),
            vmem((2, 16, SLOTS, 128), BF),
            vmem((2, 16, SLOTS, 128), BF),
            vmem((2, 2, 2, 64, 128), BF),
            vmem((8, 64, 128), BF),
            vmem((8, 256), F32),
            dma((14,)),
            dma, dma((4,)), dma, dma((2,)), dma, dma,
            *gather_sems(2),
            *gather_sems(4),
        ],
        compiler_params=pltpu.CompilerParams(
            collective_id=0, has_side_effects=True, vmem_limit_bytes=56 * 2**20
        ),
        name="decode_layer",
    )(
        queries, cache_keys, cache_values, new_keys, new_values, lengths.reshape(1, 1), residual.T, out_weight,
        norm_gain.reshape(1, 7168), router_weight.T, routes.T, jnp.swapaxes(gate_tiles, 1, 2),
        jnp.swapaxes(up_tiles, 1, 2), down_tiles,
    ).T


def solution(mesh):
    return jax.shard_map(
        local,
        mesh=mesh,
        in_specs=(
            P(("pool", "rank"), None, None),
            P(("pool", "rank"), None, None),
            P(("pool", "rank"), None, None),
            P(("pool", "rank"), None),
            P(("pool", "rank"), None),
            P(("pool", "rank")),
            P("pool", "rank"),
            P("rank", None),
            P(),
            P(),
            P(),
            P(("pool", "rank"), None, None),
            P(("pool", "rank"), None, None),
            P(("pool", "rank"), None, None),
        ),
        out_specs=P("pool", "rank"),
        check_vma=False,
    )
```

```python
import jax
import jax.numpy as jnp
from jax import lax
from jax.experimental import pallas as pl
from jax.experimental.pallas import tpu as pltpu
from jax.sharding import PartitionSpec as P

MESH = pl.DeviceIdType.MESH
BF = jnp.bfloat16
F32 = jnp.float32
EPSILON = 1e-05
SLOTS = 160
WIDE = 112
VM = pl.BlockSpec(memory_space=pltpu.VMEM)
ANY = pl.BlockSpec(memory_space=pl.ANY)


def place(rank):
    return rank // 16, lax.rem(rank // 4, 4), lax.rem(rank // 2, 2), lax.rem(rank, 2)


def rank_of(z, x, yh, c):
    return z * 16 + x * 4 + yh * 2 + c


def iota(shape, dim):
    return lax.broadcasted_iota(jnp.int32, shape, dim)


def dot(a, b):
    return jnp.dot(a, b, preferred_element_type=F32)


def wait_bytes(ref, sem):
    pltpu.make_async_copy(ref, ref, sem).wait()


def padded(tiles):
    zeros = jnp.zeros((tiles[0].shape[0], 8), tiles[0].dtype)
    out = []
    for j in range(8):
        parts = []
        for start in (WIDE * j, WIDE * j + 56):
            while start % 56 or not parts or parts[-1] is zeros:
                end = min(start // 56 * 56 + 56, start // 128 * 128 + 128)
                base = start // 128 * 128
                parts.append(tiles[start // 128][:, start - base : end - base])
                start = end
                if start % 56 == 0:
                    break
            parts.append(zeros)
        out.append(jnp.concatenate(parts, axis=1))
    return out


def lane_tile(n):
    return pl.ds(pl.multiple_of(n * 128, 128), 128)


def layer_kernel(
    queries_hbm, keys_hbm, values_hbm, new_key_hbm, new_value_hbm, length_hbm, residual_hbm,
    weight_hbm, gain_hbm, router_hbm, routes_hbm, gate_hbm, up_hbm, down_hbm, out_ref,
    new_key_ref, new_value_ref, length_ref, gain_ref, router_ref, routes_ref, queries, keys, values, residual, weight, gate, up, down, fused, cut, rows_in, rows, states,
    acc, squares, pick_ref, partial, from_core, to_group, from_group, to_rows, from_experts,
    places, load_sem, c_send, c_recv, r_send, r_recv, d_send, d_recv, *gather_sems,
):
    pool, rank = lax.axis_index("pool"), lax.axis_index("rank")
    z, x, yh, c = place(rank)
    zb = lax.rem(z, 2)
    expert = pool * 4 + z // 2
    spot = zb * 8 + x * 2 + yh
    sibling = rank + 1 - 2 * c
    same = jnp.logical_and(z // 4 == zb, lax.rem(z // 2, 2) == c)

    def member(spot_of, core):
        return (z // 2) * 32 + spot_of * 2 + core

    def copy(src, dst, send, recv, p, r):
        return pltpu.make_async_remote_copy(
            src_ref=src, dst_ref=dst, send_sem=send, recv_sem=recv, device_id=(p, r),
            device_id_type=MESH,
        )

    def in_plane(d, core):
        return lax.rem(pool + d // 8, 2), z * 16 + lax.rem(x * 2 + yh + d, 8) * 2 + core

    def is_self(p, r):
        return jnp.logical_and(p == pool, r == rank)

    loads = {}
    for n, (name, src, dst) in enumerate((
        ("queries", queries_hbm.at[0], queries), ("keys", keys_hbm.at[0], keys),
        ("new_key", new_key_hbm, new_key_ref), ("length", length_hbm, length_ref),
        ("values", values_hbm.at[0], values), ("new_value", new_value_hbm, new_value_ref),
        ("gain", gain_hbm, gain_ref), ("router", router_hbm, router_ref),
        ("gate", gate_hbm.at[0], gate), ("up", up_hbm.at[0], up), ("down", down_hbm.at[0], down),
        ("weight", weight_hbm, weight), ("residual", residual_hbm, residual),
        ("routes", routes_hbm, routes_ref),
    )):
        loads[name] = pltpu.make_async_copy(src, dst, load_sem.at[n])
        loads[name].start()

    def loaded(*names):
        for name in names:
            loads[name].wait()

    barrier = pltpu.get_barrier_semaphore()

    def greet(p, r):
        pl.semaphore_signal(barrier, inc=1, device_id=(p, r), device_id_type=MESH)

    @pl.when(c == 0)
    def _():
        for d in range(15, 0, -1):
            for core in range(2):
                greet(*in_plane(d, core))
        for n in (1, 7):
            greet(pool, rank_of(lax.rem(z + n, 8), x, yh, 0))

    @pl.when(c == 1)
    def _():
        for d in (4, 3, 5, 2, 6, 1, 7):
            for core in range(2):
                greet(pool, rank_of(lax.rem(z + d, 8), x, yh, core))
        for n in (1, 3):
            greet(pool, rank_of(z, lax.rem(x + n, 4), yh, 1))
        greet(pool, rank_of(z, x, 1 - yh, 1))
        greet(1 - pool, rank)
        greet(1 - pool, rank_of(z, x, 1 - yh, 1))

    greet(pool, sibling)

    loaded("queries", "keys", "new_key", "length")
    q = queries[...]
    scores = lax.dot_general(
        q, keys[...], (((1,), (1,)), ((), ())), preferred_element_type=F32
    ) * (1.0 / 16.0)
    self_score = jnp.sum(
        q.astype(F32) * new_key_ref[...].astype(F32), axis=1, keepdims=True
    ) * (1.0 / 16.0)
    scores = jnp.where(iota((64, 2048), 1) < length_ref[...], scores, -1e30)
    highest = jnp.maximum(jnp.max(scores, axis=1, keepdims=True), self_score)
    raised = jnp.exp(scores - highest)
    raised_self = jnp.exp(self_score - highest)
    denominator = jnp.sum(raised, axis=1, keepdims=True) + raised_self
    weights = (raised / denominator).astype(BF)
    weight_self = (raised_self / denominator).astype(BF).astype(F32)
    loaded("values", "new_value")
    context = dot(weights, values[...]) + weight_self * new_value_ref[...].astype(F32)
    context = context.astype(BF)
    rows_in[z, x, yh, c, 0:64, :] = context[:, 0:128]
    rows_in[z, x, yh, c, 64:128, :] = context[:, 128:256]

    loaded("routes")
    rows8 = iota((8, 256), 0)
    members = jnp.zeros((8, 256), F32)
    for k in range(3):
        members += (routes_ref[k : k + 1, :] == rows8).astype(F32)
    r0, r1 = iota((256, 256), 0), iota((256, 256), 1)
    order = dot(members.astype(BF), (r0 < r1).astype(BF))
    places[...] = jnp.where(members > 0.5, order, -1.0)
    acc[...] = jnp.zeros_like(acc)
    squares[...] = jnp.zeros_like(squares)
    own_places = places[pl.ds(expert, 1), :]
    pick_ref[...] = (own_places == iota((SLOTS, 256), 0).astype(F32)).astype(BF)

    pl.semaphore_wait(barrier, 25 + 3 * c)

    def gather(buf, ny, w, part, device, sems, aside, work):
        (
            p_send, p_in, o_send, z_send, z_in, ring, up_in, down_in, y_send, y_in, x_send, l_in,
            r_in, ll_in, rr_in, s_send, s_in,
        ) = sems
        size = buf.shape[4]
        first, second = pl.ds(0, part), pl.ds(part, size - part)
        flat = x * ny + w
        own = buf.at[z, x, w, c]

        def put(ref, send, recv, to):
            copy(ref, ref, send, recv, *to).start()

        def near(n, core):
            return device(lax.rem(z + n + 8, 8), x, w, core)

        def to_plane(d):
            f = lax.rem(flat + d, 4 * ny)
            put(own.at[first], p_send, p_in.at[flat * 2 + c], device(z, f // ny, lax.rem(f, ny), 0))

        @pl.when(c == 1)
        def _():
            put(own.at[first], o_send, p_in.at[flat * 2 + 1], device(z, x, w, 0))

        @pl.when(c == 0)
        def _():
            put(own.at[second], o_send, z_in.at[z * 2], device(z, x, w, 1))

        put(own.at[second], z_send, z_in.at[z * 2 + c], near(1, 1))
        put(own.at[second], z_send, z_in.at[z * 2 + c], near(-1, 1))
        for d in range(1, 4 * ny):
            to_plane(d)
        for n in (2, -2, 3, -3, 4):
            put(own.at[second], z_send, z_in.at[z * 2 + c], near(n, 1))

        def share(b, ref):
            put(ref, s_send, s_in.at[b], device(z, x, w, 1 - c))

        def share_near(core, rows):
            for i in range(1, ny):
                share(z, buf.at[z, x, lax.rem(w + i, ny), :, rows])
            share(z, buf.at[z, x, w, core, rows])

        def wait_plane(sem, rows, full):
            blocks = buf.reshape(64 * ny, size, 128)
            wait_bytes(blocks.at[pl.ds(0, 8 * ny if full else 8 * ny - 1), rows], sem)

        def finish(n, rows):
            for b in step_planes(n):
                wait_plane(s_in.at[b], rows, n > 0)
            work(step_planes(n))

        @pl.when(c == 0)
        def _():
            def chunk(b, q):
                return buf.at[b, lax.rem(x + (0, 1, 3, 2)[q], 4), :, :, first]

            aside(0, 0)
            for s in range(5):
                b_up, b_down = lax.rem(z + 8 - s, 8), lax.rem(z + s, 8)
                for q in range(4):
                    up_now, down_now = s < 4 or q < 2, s < 4 or q >= 2
                    if s == 0:
                        xx = lax.rem(x + (0, 1, 3, 2)[q], 4)
                        for i in range(ny):
                            ww = lax.rem(w + i, ny)
                            for core in range(2):
                                if q or i or core:
                                    wait_bytes(buf.at[z, xx, ww, core, first], p_in.at[(xx * ny + ww) * 2 + core])
                    if s > 0 and up_now:
                        wait_bytes(chunk(b_up, q), up_in.at[s - 1, q])
                    if s < 3 or (s == 3 and q < 2):
                        put(chunk(b_up, q), ring.at[0], up_in.at[s, q], near(1, 0))
                    if s > 0 and down_now:
                        wait_bytes(chunk(b_down, q), down_in.at[s - 1, q])
                    if s < 3 or (s == 3 and q >= 2):
                        put(chunk(b_down, q), ring.at[1], down_in.at[s, q], near(-1, 0))
                    if s == 0 and q == 0:
                        share_near(0, first)
                    elif s == 0 or up_now:
                        share(b_up, chunk(b_up, q))
                    if s > 0 and down_now:
                        share(b_down, chunk(b_down, q))
                if s < 4:
                    aside(0, s + 1)
            for n in range(5):
                finish(n, second)

            def ring_sent(n, _):
                for way in range(2):
                    wait_bytes(chunk(n, 0), ring.at[way])
                    wait_bytes(chunk(n, 0), ring.at[way])
                return 0

            lax.fori_loop(0, 7, ring_sent, 0)
            for n in range(8):
                wait_plane(s_send, first, n > 0)
            wait_bytes(own.at[second], o_send)

        @pl.when(c == 1)
        def _():
            left, right = device(z, lax.rem(x + 3, 4), w, 1), device(z, lax.rem(x + 1, 4), w, 1)
            lx, rx, ox = lax.rem(x + 3, 4), lax.rem(x + 1, 4), lax.rem(x + 2, 4)

            def along_z(n):
                for b in step_planes(n):
                    for core in range(2):
                        if n or core == 0:
                            wait_bytes(buf.at[b, x, w, core, second], z_in.at[b * 2 + core])
                    line = buf.at[b, x, w, :, second]
                    for i in range(1, ny):
                        put(line, y_send, y_in.at[b], device(z, x, lax.rem(w + i, ny), 1))

            def along_y(n):
                for b in step_planes(n):
                    wait_bytes(buf.at[b, x, pl.ds(0, ny - 1), :, second], y_in.at[b])
                    face = buf.at[b, x, :, :, second]
                    put(face, x_send, l_in.at[b], right)
                    put(face, x_send, r_in.at[b], left)
                    if n:
                        share(b, face)
                    else:
                        share_near(1, second)

            def along_x(n):
                for b in step_planes(n):
                    face = buf.at[b, lx, :, :, second]
                    wait_bytes(face, l_in.at[b])
                    put(buf.at[b, lx, pl.ds(0, ny // 2), :, second], x_send, ll_in.at[b], right)
                    share(b, face)
                    face = buf.at[b, rx, :, :, second]
                    wait_bytes(face, r_in.at[b])
                    put(buf.at[b, rx, pl.ds(ny // 2, ny // 2), :, second], x_send, rr_in.at[b], left)
                    share(b, face)

            def opposite(n):
                for b in step_planes(n):
                    wait_bytes(buf.at[b, ox, pl.ds(0, ny // 2), :, second], ll_in.at[b])
                    wait_bytes(buf.at[b, ox, pl.ds(ny // 2, ny // 2), :, second], rr_in.at[b])
                    share(b, buf.at[b, ox, :, :, second])

            aside(1, 0)
            along_z(0)
            along_z(1)
            along_y(0)
            for n in (2, 3, 4):
                along_z(n)
            aside(1, 1)
            along_y(1)
            along_y(2)
            aside(1, 2)
            along_y(3)
            along_y(4)
            along_x(0)
            along_x(1)
            aside(1, 3)
            for n in (2, 3, 4):
                along_x(n)
            for n in range(5):
                opposite(n)
            for n in range(5):
                finish(n, first)

            def line_sent(n, _):
                wait_bytes(buf.at[n, x, pl.ds(0, ny - 1), :, second], y_send)
                wait_bytes(buf.at[n, pl.ds(0, 3), :, :, second], x_send)
                return 0

            lax.fori_loop(0, 8, line_sent, 0)
            for n in range(8):
                wait_plane(s_send, second, n > 0)
            wait_bytes(own.at[first], o_send)

        def plane_sent(d, _):
            wait_bytes(own.at[first], p_send)
            return 0

        def line_sent(d, _):
            wait_bytes(own.at[second], z_send)
            return 0

        lax.fori_loop(1, 4 * ny, plane_sent, 0)
        lax.fori_loop(1, 8, line_sent, 0)

    def step_planes(s):
        if s in (0, 4):
            return [lax.rem(z + s, 8)]
        return [lax.rem(z + 8 - s, 8), lax.rem(z + s, 8)]

    def prepare(b, _):
        gains = padded([gain_ref[:, lane_tile(b * 7 + j)] for j in range(7)])
        routers = padded([router_ref[:, lane_tile(b * 7 + j)].astype(F32) for j in range(7)])
        for j in range(8):
            part = (routers[j] * gains[j]).astype(BF)
            fused[320:336, lane_tile(b * 8 + j)] = jnp.concatenate([part, jnp.zeros_like(part)], axis=0)

        def strip(n, _):
            r = pl.ds(pl.multiple_of(n * 32, 32), 32)
            for src, first in ((gate, 0), (up, SLOTS)):
                tiles = padded([src[r, lane_tile(b * 7 + j)] for j in range(7)])
                to = pl.ds(pl.multiple_of(first + n * 32, 32), 32)
                for j in range(8):
                    fused[to, lane_tile(b * 8 + j)] = (tiles[j].astype(F32) * gains[j]).astype(BF)
            tiles = padded([down[r, lane_tile(b * 7 + j)] for j in range(7)])
            for j in range(8):
                cut[r, lane_tile(b * 8 + j)] = tiles[j]
            return 0

        lax.fori_loop(0, 5, strip, 0)
        return 0

    def turn(b):
        def part(k, _):
            block = rows_in[b, :, :, :, pl.ds(pl.multiple_of(k * 16, 16), 16), :]
            block = jnp.swapaxes(block.reshape(16, 16, 128), 0, 1)
            for j in range(16):
                n = 2 * (lax.rem(k, 4) * 16 + j) + k // 4
                rows[b, :, lane_tile(n)] = block[j]
            return 0

        lax.fori_loop(0, 8, part, 0)

    def row_aside(core, n):
        if n == 0:
            loaded("gain", "router", "gate", "up", "down")
        bounds = ((0, 2, 3, 5, 7, 8), (0, 3, 5, 7, 8))[core]
        lax.fori_loop(bounds[n], bounds[n + 1], prepare, 0)

    def row_work(planes):
        for b in planes:
            turn(b)

    def row_device(dz, dx, dw, core):
        return pool, rank_of(dz, dx, dw, core)

    gather(rows_in, 2, yh, 48, row_device, gather_sems[:17], row_aside, row_work)

    loaded("weight", "residual")
    projected = lax.dot_general(
        weight[...], rows[...].reshape(128, 16384), (((1,), (1,)), ((), ())),
        preferred_element_type=F32,
    )
    hstate = (residual[...].astype(F32) + projected).astype(BF).astype(F32)
    states[z, x, yh * 2 + pool, c] = jnp.concatenate(
        [hstate, jnp.zeros((8, 128), F32)], axis=0
    ).astype(BF)

    def state_work(planes):
        for b in planes:
            k = pl.ds(pl.multiple_of(b * 1024, 1024), 1024)
            for p in range(2):
                part = jnp.concatenate(
                    [states[b, n // 2, (n % 2) * 2 + p].reshape(128, 128) for n in range(8)], axis=0
                )
                lanes = slice(p * 128, p * 128 + 128)
                acc[:, lanes] += dot(fused[:, k], part)
                wide = part.astype(F32)
                squares[:, lanes] += jnp.sum((wide * wide).reshape(128, 8, 128), axis=0)

    def state_device(dz, dx, dw, core):
        return lax.rem(dw, 2), rank_of(dz, dx, dw // 2, core)

    gather(
        states, 4, yh * 2 + pool, 32, state_device, gather_sems[17:], lambda core, n: None, state_work
    )

    pick = pick_ref[...]
    members = (places[...] >= 0.0).astype(F32)
    inv = lax.rsqrt(jnp.sum(squares[...], axis=0, keepdims=True) * (1.0 / 7168) + EPSILON)
    chosen = jax.nn.sigmoid(acc[320:328, :] * inv)
    named = jnp.where(members > 0.5, chosen, 0.0)
    whole = jnp.sum(named, axis=0, keepdims=True)
    row_share = jnp.sum(jnp.where(rows8 == expert, named, 0.0), axis=0, keepdims=True) / whole
    hidden_t = (jax.nn.silu(acc[0:160, :] * inv) * (acc[160:320, :] * inv)).astype(BF)
    hidden = lax.dot_general(
        pick, hidden_t, (((1,), (1,)), ((), ())), preferred_element_type=F32
    ).astype(BF)
    share = jnp.sum(jnp.where(pick.astype(F32) > 0.5, row_share, 0.0), axis=1, keepdims=True)

    def product(core, g, i):
        b = 4 * g + 2 * core + i
        k = pl.ds(pl.multiple_of(b * 1024, 1024), 1024)
        sums = (dot(hidden, cut[:, k]) * share).astype(BF)
        for j in range(8):
            partial[core, i, g, j] = sums[:, j * 128 : j * 128 + 128]

    def for_other(g, i):
        product(1 - c, g, i)
        copy(
            partial.at[1 - c, i, g], from_core.at[i, g], c_send, c_recv.at[2 * i + g], pool, sibling
        ).start()

    def send_sums(g, i):
        wait_bytes(from_core.at[i, g], c_recv.at[2 * i + g])

        def one(j, _):
            to = g * 8 + j
            both = (partial[c, i, g, j].astype(F32) + from_core[i, g, j].astype(F32)).astype(BF)

            @pl.when(to == spot)
            def _():
                from_group[i, to] = both

            @pl.when(to != spot)
            def _():
                to_group[i, to] = both
                copy(
                    to_group.at[i, to], from_group.at[i, spot], r_send, r_recv.at[i], pool,
                    member(to, c),
                ).start()

            return 0

        lax.fori_loop(0, 8, one, 0)

    parts = ((0, 0), (1, 0), (0, 1), (1, 1))
    for_other(*parts[0])
    for_other(*parts[1])
    product(c, *parts[0])
    for n in range(4):
        if n < 2:
            for_other(*parts[n + 2])
        if n < 3:
            product(c, *parts[n + 1])
        send_sums(*parts[n])

    for i in range(2):
        wait_bytes(from_group.at[i, pl.ds(0, 15)], r_recv.at[i])
        total = from_group[i, 0].astype(F32)
        for s in range(1, 16):
            total += from_group[i, s].astype(F32)
        spread = lax.dot_general(
            total.astype(BF), pick, (((0,), (0,)), ((), ())), preferred_element_type=F32
        ).astype(BF)
        for p in range(2):
            for core in range(2):
                to_rows[i, p, core] = spread[core * 64 : core * 64 + 64, p * 128 : p * 128 + 128]
        for p in range(2):
            for core in range(2):
                r = rank_of(4 * zb + 2 * c + i, x, yh, core)
                src, dst = to_rows.at[i, p, core], from_experts.at[expert]
                here = is_self(p, r)

                @pl.when(here)
                def _():
                    pltpu.make_async_copy(src, dst, d_recv).start()

                @pl.when(jnp.logical_not(here))
                def _():
                    copy(src, dst, d_send, d_recv, p, r).start()

    wait_bytes(from_experts, d_recv)
    sums = from_experts[0].astype(F32)
    for e in range(1, 8):
        sums += from_experts[e].astype(F32)
    out_ref[...] = (hstate + sums[0:56]).astype(BF)

    wait_bytes(from_core, c_send)
    wait_bytes(from_group.at[:, pl.ds(0, 15)], r_send)
    wait_bytes(from_experts.at[pl.ds(0, 7)], d_send)

    @pl.when(jnp.logical_not(same))
    def _():
        wait_bytes(from_experts.at[0], d_send)


def local(
    queries, cache_keys, cache_values, new_keys, new_values, lengths, residual, out_weight,
    norm_gain, router_weight, routes, gate_tiles, up_tiles, down_tiles,
):
    dma = pltpu.SemaphoreType.DMA
    vmem = pltpu.VMEM

    def gather_sems(ny):
        return [
            dma, dma((8 * ny,)), dma, dma, dma((16,)), dma((2,)), dma((4, 4)), dma((4, 4)), dma,
            dma((8,)), dma, dma((8,)), dma((8,)), dma((8,)), dma((8,)), dma, dma((8,)),
        ]

    return pl.pallas_call(
        layer_kernel,
        out_shape=jax.ShapeDtypeStruct((56, 128), BF),
        in_specs=[
            ANY, ANY, ANY, ANY, ANY, ANY, ANY, ANY, ANY, ANY, ANY, ANY, ANY, ANY,
        ],
        out_specs=VM,
        scratch_shapes=[
            vmem((1, 256), BF),
            vmem((1, 256), BF),
            vmem((1, 1), jnp.int32),
            vmem((1, 7168), F32),
            vmem((8, 7168), BF),
            vmem((3, 256), jnp.int32),
            vmem((64, 256), BF),
            vmem((2048, 256), BF),
            vmem((2048, 256), BF),
            vmem((56, 128), BF),
            vmem((56, 16384), BF),
            vmem((SLOTS, 7168), BF),
            vmem((SLOTS, 7168), BF),
            vmem((SLOTS, 7168), BF),
            vmem((336, 8192), BF),
            vmem((SLOTS, 8192), BF),
            vmem((8, 4, 2, 2, 128, 128), BF),
            vmem((8, 16, 16384), BF),
            vmem((8, 4, 4, 2, 64, 128), BF),
            vmem((336, 256), F32),
            vmem((8, 256), F32),
            vmem((SLOTS, 256), BF),
            vmem((2, 2, 2, 8, SLOTS, 128), BF),
            vmem((2, 2, 8, SLOTS, 128), BF),
            vmem((2, 16, SLOTS, 128), BF),
            vmem((2, 16, SLOTS, 128), BF),
            vmem((2, 2, 2, 64, 128), BF),
            vmem((8, 64, 128), BF),
            vmem((8, 256), F32),
            dma((14,)),
            dma, dma((4,)), dma, dma((2,)), dma, dma,
            *gather_sems(2),
            *gather_sems(4),
        ],
        compiler_params=pltpu.CompilerParams(
            collective_id=0, has_side_effects=True, vmem_limit_bytes=56 * 2**20
        ),
        name="decode_layer",
    )(
        queries, cache_keys, cache_values, new_keys, new_values, lengths.reshape(1, 1), residual.T, out_weight,
        norm_gain.reshape(1, 7168), router_weight.T, routes.T, jnp.swapaxes(gate_tiles, 1, 2),
        jnp.swapaxes(up_tiles, 1, 2), down_tiles,
    ).T


def solution(mesh):
    return jax.shard_map(
        local,
        mesh=mesh,
        in_specs=(
            P(("pool", "rank"), None, None),
            P(("pool", "rank"), None, None),
            P(("pool", "rank"), None, None),
            P(("pool", "rank"), None),
            P(("pool", "rank"), None),
            P(("pool", "rank")),
            P("pool", "rank"),
            P("rank", None),
            P(),
            P(),
            P(),
            P(("pool", "rank"), None, None),
            P(("pool", "rank"), None, None),
            P(("pool", "rank"), None, None),
        ),
        out_specs=P("pool", "rank"),
        check_vma=False,
    )
```

```python
import jax
import jax.numpy as jnp
from jax import lax
from jax.experimental import pallas as pl
from jax.experimental.pallas import tpu as pltpu
from jax.sharding import PartitionSpec as P

MESH = pl.DeviceIdType.MESH
BF = jnp.bfloat16
F32 = jnp.float32
EPSILON = 1e-05
SLOTS = 160
WIDE = 112
VM = pl.BlockSpec(memory_space=pltpu.VMEM)
ANY = pl.BlockSpec(memory_space=pl.ANY)


def place(rank):
    return rank // 16, lax.rem(rank // 4, 4), lax.rem(rank // 2, 2), lax.rem(rank, 2)


def rank_of(z, x, yh, c):
    return z * 16 + x * 4 + yh * 2 + c


def iota(shape, dim):
    return lax.broadcasted_iota(jnp.int32, shape, dim)


def dot(a, b):
    return jnp.dot(a, b, preferred_element_type=F32)


def wait_bytes(ref, sem):
    pltpu.make_async_copy(ref, ref, sem).wait()


def padded(tiles):
    zeros = jnp.zeros((tiles[0].shape[0], 8), tiles[0].dtype)
    out = []
    for j in range(8):
        parts = []
        for start in (WIDE * j, WIDE * j + 56):
            while start % 56 or not parts or parts[-1] is zeros:
                end = min(start // 56 * 56 + 56, start // 128 * 128 + 128)
                base = start // 128 * 128
                parts.append(tiles[start // 128][:, start - base : end - base])
                start = end
                if start % 56 == 0:
                    break
            parts.append(zeros)
        out.append(jnp.concatenate(parts, axis=1))
    return out


def lane_tile(n):
    return pl.ds(pl.multiple_of(n * 128, 128), 128)


def layer_kernel(
    queries_hbm, keys_hbm, values_hbm, new_key_hbm, new_value_hbm, length_hbm, residual_hbm,
    weight_hbm, gain_hbm, router_hbm, routes_hbm, gate_hbm, up_hbm, down_hbm, out_ref,
    new_key_ref, new_value_ref, length_ref, gain_ref, router_ref, routes_ref, queries, keys, values, residual, weight, gate, up, down, fused, cut, rows_in, rows, states,
    acc, squares, pick_ref, partial, from_core, to_group, from_group, to_rows, from_experts,
    places, load_sem, c_send, c_recv, r_send, r_recv, d_send, d_recv, *gather_sems,
):
    pool, rank = lax.axis_index("pool"), lax.axis_index("rank")
    z, x, yh, c = place(rank)
    zb = lax.rem(z, 2)
    expert = pool * 4 + z // 2
    spot = zb * 8 + x * 2 + yh
    sibling = rank + 1 - 2 * c
    same = jnp.logical_and(z // 4 == zb, lax.rem(z // 2, 2) == c)

    def member(spot_of, core):
        return (z // 2) * 32 + spot_of * 2 + core

    def copy(src, dst, send, recv, p, r):
        return pltpu.make_async_remote_copy(
            src_ref=src, dst_ref=dst, send_sem=send, recv_sem=recv, device_id=(p, r),
            device_id_type=MESH,
        )

    def in_plane(d, core):
        return lax.rem(pool + d // 8, 2), z * 16 + lax.rem(x * 2 + yh + d, 8) * 2 + core

    def is_self(p, r):
        return jnp.logical_and(p == pool, r == rank)

    loads = {}
    for n, (name, src, dst) in enumerate((
        ("queries", queries_hbm.at[0], queries), ("keys", keys_hbm.at[0], keys),
        ("new_key", new_key_hbm, new_key_ref), ("length", length_hbm, length_ref),
        ("values", values_hbm.at[0], values), ("new_value", new_value_hbm, new_value_ref),
        ("gain", gain_hbm, gain_ref), ("router", router_hbm, router_ref),
        ("gate", gate_hbm.at[0], gate), ("up", up_hbm.at[0], up), ("down", down_hbm.at[0], down),
        ("weight", weight_hbm, weight), ("residual", residual_hbm, residual),
        ("routes", routes_hbm, routes_ref),
    )):
        loads[name] = pltpu.make_async_copy(src, dst, load_sem.at[n])
        loads[name].start()

    def loaded(*names):
        for name in names:
            loads[name].wait()

    barrier = pltpu.get_barrier_semaphore()

    def greet(p, r):
        pl.semaphore_signal(barrier, inc=1, device_id=(p, r), device_id_type=MESH)

    @pl.when(c == 0)
    def _():
        for d in range(15, 0, -1):
            for core in range(2):
                greet(*in_plane(d, core))
        for n in (1, 7):
            greet(pool, rank_of(lax.rem(z + n, 8), x, yh, 0))

    @pl.when(c == 1)
    def _():
        for d in (4, 3, 5, 2, 6, 1, 7):
            for core in range(2):
                greet(pool, rank_of(lax.rem(z + d, 8), x, yh, core))
        for n in (1, 3):
            greet(pool, rank_of(z, lax.rem(x + n, 4), yh, 1))
        greet(pool, rank_of(z, x, 1 - yh, 1))
        greet(1 - pool, rank)
        greet(1 - pool, rank_of(z, x, 1 - yh, 1))

    greet(pool, sibling)

    loaded("queries", "keys", "new_key", "length")
    q = queries[...]
    scores = lax.dot_general(
        q, keys[...], (((1,), (1,)), ((), ())), preferred_element_type=F32
    ) * (1.0 / 16.0)
    self_score = jnp.sum(
        q.astype(F32) * new_key_ref[...].astype(F32), axis=1, keepdims=True
    ) * (1.0 / 16.0)
    scores = jnp.where(iota((64, 2048), 1) < length_ref[...], scores, -1e30)
    highest = jnp.maximum(jnp.max(scores, axis=1, keepdims=True), self_score)
    raised = jnp.exp(scores - highest)
    raised_self = jnp.exp(self_score - highest)
    denominator = jnp.sum(raised, axis=1, keepdims=True) + raised_self
    weights = (raised / denominator).astype(BF)
    weight_self = (raised_self / denominator).astype(BF).astype(F32)
    loaded("values", "new_value")
    context = dot(weights, values[...]) + weight_self * new_value_ref[...].astype(F32)
    context = context.astype(BF)
    rows_in[z, x, yh, c, 0:64, :] = context[:, 0:128]
    rows_in[z, x, yh, c, 64:128, :] = context[:, 128:256]

    loaded("routes")
    rows8 = iota((8, 256), 0)
    members = jnp.zeros((8, 256), F32)
    for k in range(3):
        members += (routes_ref[k : k + 1, :] == rows8).astype(F32)
    r0, r1 = iota((256, 256), 0), iota((256, 256), 1)
    order = dot(members.astype(BF), (r0 < r1).astype(BF))
    places[...] = jnp.where(members > 0.5, order, -1.0)
    acc[...] = jnp.zeros_like(acc)
    squares[...] = jnp.zeros_like(squares)
    own_places = places[pl.ds(expert, 1), :]
    pick_ref[...] = (own_places == iota((SLOTS, 256), 0).astype(F32)).astype(BF)

    def gather(buf, ny, w, part, device, sems, aside, work):
        (
            p_send, p_in, o_send, z_send, z_in, ring, up_in, down_in, y_send, y_in, x_send, l_in,
            r_in, ll_in, rr_in, s_send, s_in,
        ) = sems
        size = buf.shape[4]
        first, second = pl.ds(0, part), pl.ds(part, size - part)
        flat = x * ny + w
        own = buf.at[z, x, w, c]

        def put(ref, send, recv, to):
            copy(ref, ref, send, recv, *to).start()

        def near(n, core):
            return device(lax.rem(z + n + 8, 8), x, w, core)

        def to_plane(d):
            f = lax.rem(flat + d, 4 * ny)
            put(own.at[first], p_send, p_in.at[flat * 2 + c], device(z, f // ny, lax.rem(f, ny), 0))

        @pl.when(c == 1)
        def _():
            put(own.at[first], o_send, p_in.at[flat * 2 + 1], device(z, x, w, 0))

        @pl.when(c == 0)
        def _():
            put(own.at[second], o_send, z_in.at[z * 2], device(z, x, w, 1))

        put(own.at[second], z_send, z_in.at[z * 2 + c], near(1, 1))
        put(own.at[second], z_send, z_in.at[z * 2 + c], near(-1, 1))
        for d in range(1, 4 * ny):
            to_plane(d)
        for n in (2, -2, 3, -3, 4):
            put(own.at[second], z_send, z_in.at[z * 2 + c], near(n, 1))

        def share(b, ref):
            put(ref, s_send, s_in.at[b], device(z, x, w, 1 - c))

        def share_near(core, rows):
            for i in range(1, ny):
                share(z, buf.at[z, x, lax.rem(w + i, ny), :, rows])
            share(z, buf.at[z, x, w, core, rows])

        def wait_plane(sem, rows, full):
            blocks = buf.reshape(64 * ny, size, 128)
            wait_bytes(blocks.at[pl.ds(0, 8 * ny if full else 8 * ny - 1), rows], sem)

        def finish(n, rows):
            for b in step_planes(n):
                wait_plane(s_in.at[b], rows, n > 0)
            work(step_planes(n))

        @pl.when(c == 0)
        def _():
            def chunk(b, q):
                return buf.at[b, lax.rem(x + (0, 1, 3, 2)[q], 4), :, :, first]

            aside(0, 0)
            for s in range(5):
                b_up, b_down = lax.rem(z + 8 - s, 8), lax.rem(z + s, 8)
                for q in range(4):
                    up_now, down_now = s < 4 or q < 2, s < 4 or q >= 2
                    if s == 0:
                        xx = lax.rem(x + (0, 1, 3, 2)[q], 4)
                        for i in range(ny):
                            ww = lax.rem(w + i, ny)
                            for core in range(2):
                                if q or i or core:
                                    wait_bytes(buf.at[z, xx, ww, core, first], p_in.at[(xx * ny + ww) * 2 + core])
                    if s > 0 and up_now:
                        wait_bytes(chunk(b_up, q), up_in.at[s - 1, q])
                    if s < 3 or (s == 3 and q < 2):
                        put(chunk(b_up, q), ring.at[0], up_in.at[s, q], near(1, 0))
                    if s > 0 and down_now:
                        wait_bytes(chunk(b_down, q), down_in.at[s - 1, q])
                    if s < 3 or (s == 3 and q >= 2):
                        put(chunk(b_down, q), ring.at[1], down_in.at[s, q], near(-1, 0))
                    if s == 0 and q == 0:
                        share_near(0, first)
                    elif s == 0 or up_now:
                        share(b_up, chunk(b_up, q))
                    if s > 0 and down_now:
                        share(b_down, chunk(b_down, q))
                if s < 4:
                    aside(0, s + 1)
                if s == 3:
                    finish(0, second)
            for n in range(1, 5):
                finish(n, second)

            def ring_sent(n, _):
                for way in range(2):
                    wait_bytes(chunk(n, 0), ring.at[way])
                    wait_bytes(chunk(n, 0), ring.at[way])
                return 0

            lax.fori_loop(0, 7, ring_sent, 0)
            for n in range(8):
                wait_plane(s_send, first, n > 0)
            wait_bytes(own.at[second], o_send)

        @pl.when(c == 1)
        def _():
            left, right = device(z, lax.rem(x + 3, 4), w, 1), device(z, lax.rem(x + 1, 4), w, 1)
            lx, rx, ox = lax.rem(x + 3, 4), lax.rem(x + 1, 4), lax.rem(x + 2, 4)

            def along_z(n):
                for b in step_planes(n):
                    for core in range(2):
                        if n or core == 0:
                            wait_bytes(buf.at[b, x, w, core, second], z_in.at[b * 2 + core])
                    line = buf.at[b, x, w, :, second]
                    for i in range(1, ny):
                        put(line, y_send, y_in.at[b], device(z, x, lax.rem(w + i, ny), 1))

            def along_y(n):
                for b in step_planes(n):
                    wait_bytes(buf.at[b, x, pl.ds(0, ny - 1), :, second], y_in.at[b])
                    face = buf.at[b, x, :, :, second]
                    put(face, x_send, l_in.at[b], right)
                    put(face, x_send, r_in.at[b], left)
                    if n:
                        share(b, face)
                    else:
                        share_near(1, second)

            def along_x(n):
                for b in step_planes(n):
                    face = buf.at[b, lx, :, :, second]
                    wait_bytes(face, l_in.at[b])
                    put(buf.at[b, lx, pl.ds(0, ny // 2), :, second], x_send, ll_in.at[b], right)
                    share(b, face)
                    face = buf.at[b, rx, :, :, second]
                    wait_bytes(face, r_in.at[b])
                    put(buf.at[b, rx, pl.ds(ny // 2, ny // 2), :, second], x_send, rr_in.at[b], left)
                    share(b, face)

            def opposite(n):
                for b in step_planes(n):
                    wait_bytes(buf.at[b, ox, pl.ds(0, ny // 2), :, second], ll_in.at[b])
                    wait_bytes(buf.at[b, ox, pl.ds(ny // 2, ny // 2), :, second], rr_in.at[b])
                    share(b, buf.at[b, ox, :, :, second])

            aside(1, 0)
            along_z(0)
            along_z(1)
            along_y(0)
            for n in (2, 3, 4):
                along_z(n)
            aside(1, 1)
            along_y(1)
            along_y(2)
            aside(1, 2)
            along_y(3)
            along_y(4)
            along_x(0)
            along_x(1)
            aside(1, 3)
            for n in (2, 3, 4):
                along_x(n)
            opposite(0)
            for n in range(1, 5):
                opposite(n)
                finish(n - 1, first)
            finish(4, first)

            def line_sent(n, _):
                wait_bytes(buf.at[n, x, pl.ds(0, ny - 1), :, second], y_send)
                wait_bytes(buf.at[n, pl.ds(0, 3), :, :, second], x_send)
                return 0

            lax.fori_loop(0, 8, line_sent, 0)
            for n in range(8):
                wait_plane(s_send, second, n > 0)
            wait_bytes(own.at[first], o_send)

        def plane_sent(d, _):
            wait_bytes(own.at[first], p_send)
            return 0

        def line_sent(d, _):
            wait_bytes(own.at[second], z_send)
            return 0

        lax.fori_loop(1, 4 * ny, plane_sent, 0)
        lax.fori_loop(1, 8, line_sent, 0)

    def step_planes(s):
        if s in (0, 4):
            return [lax.rem(z + s, 8)]
        return [lax.rem(z + 8 - s, 8), lax.rem(z + s, 8)]

    def prepare(b, _):
        gains = padded([gain_ref[:, lane_tile(b * 7 + j)] for j in range(7)])
        routers = padded([router_ref[:, lane_tile(b * 7 + j)].astype(F32) for j in range(7)])
        for j in range(8):
            part = (routers[j] * gains[j]).astype(BF)
            fused[320:336, lane_tile(b * 8 + j)] = jnp.concatenate([part, jnp.zeros_like(part)], axis=0)

        def strip(n, _):
            r = pl.ds(pl.multiple_of(n * 32, 32), 32)
            for src, first in ((gate, 0), (up, SLOTS)):
                tiles = padded([src[r, lane_tile(b * 7 + j)] for j in range(7)])
                to = pl.ds(pl.multiple_of(first + n * 32, 32), 32)
                for j in range(8):
                    fused[to, lane_tile(b * 8 + j)] = (tiles[j].astype(F32) * gains[j]).astype(BF)
            return 0

        lax.fori_loop(0, 5, strip, 0)
        return 0

    def prepare_down(b, _):
        def strip(n, _):
            r = pl.ds(pl.multiple_of(n * 32, 32), 32)
            tiles = padded([down[r, lane_tile(b * 7 + j)] for j in range(7)])
            for j in range(8):
                cut[r, lane_tile(b * 8 + j)] = tiles[j]
            return 0

        lax.fori_loop(0, 5, strip, 0)
        return 0

    def turn(b):
        def part(k, _):
            block = rows_in[b, :, :, :, pl.ds(pl.multiple_of(k * 16, 16), 16), :]
            block = jnp.swapaxes(block.reshape(16, 16, 128), 0, 1)
            for j in range(16):
                n = 2 * (lax.rem(k, 4) * 16 + j) + k // 4
                rows[b, :, lane_tile(n)] = block[j]
            return 0

        lax.fori_loop(0, 8, part, 0)

    def row_aside(core, n):
        first = (2, 2)[core] if n == 0 else ((4, 5, 6, 7), (5, 8, 8))[core][n - 1]
        last = ((4, 5, 6, 7, 8), (5, 8, 8, 8))[core][n]
        if first < last:
            lax.fori_loop(first, last, prepare, 0)

    def row_work(planes):
        for b in planes:
            turn(b)

    def row_device(dz, dx, dw, core):
        return pool, rank_of(dz, dx, dw, core)

    loaded("gain", "router", "gate", "up")
    lax.fori_loop(0, 2, prepare, 0)
    pl.semaphore_wait(barrier, 25 + 3 * c)
    gather(rows_in, 2, yh, 48, row_device, gather_sems[:17], row_aside, row_work)

    loaded("weight", "residual")
    projected = lax.dot_general(
        weight[...], rows[...].reshape(128, 16384), (((1,), (1,)), ((), ())),
        preferred_element_type=F32,
    )
    hstate = (residual[...].astype(F32) + projected).astype(BF).astype(F32)
    states[z, x, yh * 2 + pool, c] = jnp.concatenate(
        [hstate, jnp.zeros((8, 128), F32)], axis=0
    ).astype(BF)

    def state_work(planes):
        for b in planes:
            k = pl.ds(pl.multiple_of(b * 1024, 1024), 1024)
            for p in range(2):
                part = jnp.concatenate(
                    [states[b, n // 2, (n % 2) * 2 + p].reshape(128, 128) for n in range(8)], axis=0
                )
                lanes = slice(p * 128, p * 128 + 128)
                acc[:, lanes] += dot(fused[:, k], part)
                wide = part.astype(F32)
                squares[:, lanes] += jnp.sum((wide * wide).reshape(128, 8, 128), axis=0)

    def state_aside(core, n):
        if n == 0:
            loaded("down")
        first = 0 if n == 0 else ((3, 5, 6, 7), (4, 8, 8))[core][n - 1]
        last = ((3, 5, 6, 7, 8), (4, 8, 8, 8))[core][n]
        if first < last:
            lax.fori_loop(first, last, prepare_down, 0)

    def state_device(dz, dx, dw, core):
        return lax.rem(dw, 2), rank_of(dz, dx, dw // 2, core)

    gather(
        states, 4, yh * 2 + pool, 32, state_device, gather_sems[17:], state_aside, state_work
    )

    pick = pick_ref[...]
    members = (places[...] >= 0.0).astype(F32)
    inv = lax.rsqrt(jnp.sum(squares[...], axis=0, keepdims=True) * (1.0 / 7168) + EPSILON)
    chosen = jax.nn.sigmoid(acc[320:328, :] * inv)
    named = jnp.where(members > 0.5, chosen, 0.0)
    whole = jnp.sum(named, axis=0, keepdims=True)
    row_share = jnp.sum(jnp.where(rows8 == expert, named, 0.0), axis=0, keepdims=True) / whole
    hidden_t = (jax.nn.silu(acc[0:160, :] * inv) * (acc[160:320, :] * inv)).astype(BF)
    hidden = lax.dot_general(
        pick, hidden_t, (((1,), (1,)), ((), ())), preferred_element_type=F32
    ).astype(BF)
    share = jnp.sum(jnp.where(pick.astype(F32) > 0.5, row_share, 0.0), axis=1, keepdims=True)

    def product(core, g, i):
        b = 4 * g + 2 * core + i
        k = pl.ds(pl.multiple_of(b * 1024, 1024), 1024)
        sums = (dot(hidden, cut[:, k]) * share).astype(BF)
        for j in range(8):
            partial[core, i, g, j] = sums[:, j * 128 : j * 128 + 128]

    def for_other(g, i):
        product(1 - c, g, i)
        copy(
            partial.at[1 - c, i, g], from_core.at[i, g], c_send, c_recv.at[2 * i + g], pool, sibling
        ).start()

    def send_sums(g, i):
        wait_bytes(from_core.at[i, g], c_recv.at[2 * i + g])

        def one(j, _):
            to = g * 8 + j
            both = (partial[c, i, g, j].astype(F32) + from_core[i, g, j].astype(F32)).astype(BF)

            @pl.when(to == spot)
            def _():
                from_group[i, to] = both

            @pl.when(to != spot)
            def _():
                to_group[i, to] = both
                copy(
                    to_group.at[i, to], from_group.at[i, spot], r_send, r_recv.at[i], pool,
                    member(to, c),
                ).start()

            return 0

        lax.fori_loop(0, 8, one, 0)

    parts = ((0, 0), (1, 0), (0, 1), (1, 1))
    for_other(*parts[0])
    for_other(*parts[1])
    product(c, *parts[0])
    for n in range(4):
        if n < 2:
            for_other(*parts[n + 2])
        if n < 3:
            product(c, *parts[n + 1])
        send_sums(*parts[n])

    for i in range(2):
        wait_bytes(from_group.at[i, pl.ds(0, 15)], r_recv.at[i])
        total = from_group[i, 0].astype(F32)
        for s in range(1, 16):
            total += from_group[i, s].astype(F32)
        spread = lax.dot_general(
            total.astype(BF), pick, (((0,), (0,)), ((), ())), preferred_element_type=F32
        ).astype(BF)
        for p in range(2):
            for core in range(2):
                to_rows[i, p, core] = spread[core * 64 : core * 64 + 64, p * 128 : p * 128 + 128]
        for p in range(2):
            for core in range(2):
                r = rank_of(4 * zb + 2 * c + i, x, yh, core)
                src, dst = to_rows.at[i, p, core], from_experts.at[expert]
                here = is_self(p, r)

                @pl.when(here)
                def _():
                    pltpu.make_async_copy(src, dst, d_recv).start()

                @pl.when(jnp.logical_not(here))
                def _():
                    copy(src, dst, d_send, d_recv, p, r).start()

    wait_bytes(from_experts, d_recv)
    sums = from_experts[0].astype(F32)
    for e in range(1, 8):
        sums += from_experts[e].astype(F32)
    out_ref[...] = (hstate + sums[0:56]).astype(BF)

    wait_bytes(from_core, c_send)
    wait_bytes(from_group.at[:, pl.ds(0, 15)], r_send)
    wait_bytes(from_experts.at[pl.ds(0, 7)], d_send)

    @pl.when(jnp.logical_not(same))
    def _():
        wait_bytes(from_experts.at[0], d_send)


def local(
    queries, cache_keys, cache_values, new_keys, new_values, lengths, residual, out_weight,
    norm_gain, router_weight, routes, gate_tiles, up_tiles, down_tiles,
):
    dma = pltpu.SemaphoreType.DMA
    vmem = pltpu.VMEM

    def gather_sems(ny):
        return [
            dma, dma((8 * ny,)), dma, dma, dma((16,)), dma((2,)), dma((4, 4)), dma((4, 4)), dma,
            dma((8,)), dma, dma((8,)), dma((8,)), dma((8,)), dma((8,)), dma, dma((8,)),
        ]

    return pl.pallas_call(
        layer_kernel,
        out_shape=jax.ShapeDtypeStruct((56, 128), BF),
        in_specs=[
            ANY, ANY, ANY, ANY, ANY, ANY, ANY, ANY, ANY, ANY, ANY, ANY, ANY, ANY,
        ],
        out_specs=VM,
        scratch_shapes=[
            vmem((1, 256), BF),
            vmem((1, 256), BF),
            vmem((1, 1), jnp.int32),
            vmem((1, 7168), F32),
            vmem((8, 7168), BF),
            vmem((3, 256), jnp.int32),
            vmem((64, 256), BF),
            vmem((2048, 256), BF),
            vmem((2048, 256), BF),
            vmem((56, 128), BF),
            vmem((56, 16384), BF),
            vmem((SLOTS, 7168), BF),
            vmem((SLOTS, 7168), BF),
            vmem((SLOTS, 7168), BF),
            vmem((336, 8192), BF),
            vmem((SLOTS, 8192), BF),
            vmem((8, 4, 2, 2, 128, 128), BF),
            vmem((8, 16, 16384), BF),
            vmem((8, 4, 4, 2, 64, 128), BF),
            vmem((336, 256), F32),
            vmem((8, 256), F32),
            vmem((SLOTS, 256), BF),
            vmem((2, 2, 2, 8, SLOTS, 128), BF),
            vmem((2, 2, 8, SLOTS, 128), BF),
            vmem((2, 16, SLOTS, 128), BF),
            vmem((2, 16, SLOTS, 128), BF),
            vmem((2, 2, 2, 64, 128), BF),
            vmem((8, 64, 128), BF),
            vmem((8, 256), F32),
            dma((14,)),
            dma, dma((4,)), dma, dma((2,)), dma, dma,
            *gather_sems(2),
            *gather_sems(4),
        ],
        compiler_params=pltpu.CompilerParams(
            collective_id=0, has_side_effects=True, vmem_limit_bytes=56 * 2**20
        ),
        name="decode_layer",
    )(
        queries, cache_keys, cache_values, new_keys, new_values, lengths.reshape(1, 1), residual.T, out_weight,
        norm_gain.reshape(1, 7168), router_weight.T, routes.T, jnp.swapaxes(gate_tiles, 1, 2),
        jnp.swapaxes(up_tiles, 1, 2), down_tiles,
    ).T


def solution(mesh):
    return jax.shard_map(
        local,
        mesh=mesh,
        in_specs=(
            P(("pool", "rank"), None, None),
            P(("pool", "rank"), None, None),
            P(("pool", "rank"), None, None),
            P(("pool", "rank"), None),
            P(("pool", "rank"), None),
            P(("pool", "rank")),
            P("pool", "rank"),
            P("rank", None),
            P(),
            P(),
            P(),
            P(("pool", "rank"), None, None),
            P(("pool", "rank"), None, None),
            P(("pool", "rank"), None, None),
        ),
        out_specs=P("pool", "rank"),
        check_vma=False,
    )
```

```python
import jax
import jax.numpy as jnp
from jax import lax
from jax.experimental import pallas as pl
from jax.experimental.pallas import tpu as pltpu
from jax.sharding import PartitionSpec as P

MESH = pl.DeviceIdType.MESH
BF = jnp.bfloat16
F32 = jnp.float32
EPSILON = 1e-05
SLOTS = 160
WIDE = 112
VM = pl.BlockSpec(memory_space=pltpu.VMEM)
ANY = pl.BlockSpec(memory_space=pl.ANY)


def place(rank):
    return rank // 16, lax.rem(rank // 4, 4), lax.rem(rank // 2, 2), lax.rem(rank, 2)


def rank_of(z, x, yh, c):
    return z * 16 + x * 4 + yh * 2 + c


def iota(shape, dim):
    return lax.broadcasted_iota(jnp.int32, shape, dim)


def dot(a, b):
    return jnp.dot(a, b, preferred_element_type=F32)


def wait_bytes(ref, sem):
    pltpu.make_async_copy(ref, ref, sem).wait()


def padded(tiles):
    zeros = jnp.zeros((tiles[0].shape[0], 8), tiles[0].dtype)
    out = []
    for j in range(8):
        parts = []
        for start in (WIDE * j, WIDE * j + 56):
            while start % 56 or not parts or parts[-1] is zeros:
                end = min(start // 56 * 56 + 56, start // 128 * 128 + 128)
                base = start // 128 * 128
                parts.append(tiles[start // 128][:, start - base : end - base])
                start = end
                if start % 56 == 0:
                    break
            parts.append(zeros)
        out.append(jnp.concatenate(parts, axis=1))
    return out


def lane_tile(n):
    return pl.ds(pl.multiple_of(n * 128, 128), 128)


def layer_kernel(
    queries_hbm, keys_hbm, values_hbm, new_key_hbm, new_value_hbm, length_hbm, residual_hbm,
    weight_hbm, gain_hbm, router_hbm, routes_hbm, gate_hbm, up_hbm, down_hbm, out_ref,
    new_key_ref, new_value_ref, length_ref, gain_ref, router_ref, routes_ref, queries, keys, values, residual, weight, gate, up, down, fused, cut, rows_in, rows, states,
    acc, squares, pick_ref, partial, from_core, to_group, from_group, to_rows, from_experts,
    places, load_sem, c_send, c_recv, r_send, r_recv, d_send, d_recv, *gather_sems,
):
    pool, rank = lax.axis_index("pool"), lax.axis_index("rank")
    z, x, yh, c = place(rank)
    zb = lax.rem(z, 2)
    expert = pool * 4 + z // 2
    spot = zb * 8 + x * 2 + yh
    sibling = rank + 1 - 2 * c
    same = jnp.logical_and(z // 4 == zb, lax.rem(z // 2, 2) == c)

    def member(spot_of, core):
        return (z // 2) * 32 + spot_of * 2 + core

    def copy(src, dst, send, recv, p, r):
        return pltpu.make_async_remote_copy(
            src_ref=src, dst_ref=dst, send_sem=send, recv_sem=recv, device_id=(p, r),
            device_id_type=MESH,
        )

    def in_plane(d, core):
        return lax.rem(pool + d // 8, 2), z * 16 + lax.rem(x * 2 + yh + d, 8) * 2 + core

    def is_self(p, r):
        return jnp.logical_and(p == pool, r == rank)

    loads = {}
    for n, (name, src, dst) in enumerate((
        ("queries", queries_hbm.at[0], queries), ("keys", keys_hbm.at[0], keys),
        ("new_key", new_key_hbm, new_key_ref), ("length", length_hbm, length_ref),
        ("values", values_hbm.at[0], values), ("new_value", new_value_hbm, new_value_ref),
        ("gain", gain_hbm, gain_ref), ("router", router_hbm, router_ref),
        ("gate", gate_hbm.at[0], gate), ("up", up_hbm.at[0], up), ("down", down_hbm.at[0], down),
        ("weight", weight_hbm, weight), ("residual", residual_hbm, residual),
        ("routes", routes_hbm, routes_ref),
    )):
        loads[name] = pltpu.make_async_copy(src, dst, load_sem.at[n])
        loads[name].start()

    def loaded(*names):
        for name in names:
            loads[name].wait()

    barrier = pltpu.get_barrier_semaphore()

    def greet(p, r):
        pl.semaphore_signal(barrier, inc=1, device_id=(p, r), device_id_type=MESH)

    @pl.when(c == 0)
    def _():
        for d in range(15, 0, -1):
            for core in range(2):
                greet(*in_plane(d, core))
        for n in (1, 7):
            greet(pool, rank_of(lax.rem(z + n, 8), x, yh, 0))

    @pl.when(c == 1)
    def _():
        for d in (4, 3, 5, 2, 6, 1, 7):
            for core in range(2):
                greet(pool, rank_of(lax.rem(z + d, 8), x, yh, core))
        for n in (1, 3):
            greet(pool, rank_of(z, lax.rem(x + n, 4), yh, 1))
        greet(pool, rank_of(z, x, 1 - yh, 1))
        greet(1 - pool, rank)
        greet(1 - pool, rank_of(z, x, 1 - yh, 1))

    greet(pool, sibling)

    loaded("queries", "keys", "new_key", "length")
    q = queries[...]
    scores = lax.dot_general(
        q, keys[...], (((1,), (1,)), ((), ())), preferred_element_type=F32
    ) * (1.0 / 16.0)
    self_score = jnp.sum(
        q.astype(F32) * new_key_ref[...].astype(F32), axis=1, keepdims=True
    ) * (1.0 / 16.0)
    scores = jnp.where(iota((64, 2048), 1) < length_ref[...], scores, -1e30)
    highest = jnp.maximum(jnp.max(scores, axis=1, keepdims=True), self_score)
    raised = jnp.exp(scores - highest)
    raised_self = jnp.exp(self_score - highest)
    denominator = jnp.sum(raised, axis=1, keepdims=True) + raised_self
    weights = (raised / denominator).astype(BF)
    weight_self = (raised_self / denominator).astype(BF).astype(F32)
    loaded("values", "new_value")
    context = dot(weights, values[...]) + weight_self * new_value_ref[...].astype(F32)
    context = context.astype(BF)
    rows_in[z, x, yh, c, 0:64, :] = context[:, 0:128]
    rows_in[z, x, yh, c, 64:128, :] = context[:, 128:256]

    loaded("routes")
    rows8 = iota((8, 256), 0)
    members = jnp.zeros((8, 256), F32)
    for k in range(3):
        members += (routes_ref[k : k + 1, :] == rows8).astype(F32)
    r0, r1 = iota((256, 256), 0), iota((256, 256), 1)
    order = dot(members.astype(BF), (r0 < r1).astype(BF))
    places[...] = jnp.where(members > 0.5, order, -1.0)
    acc[...] = jnp.zeros_like(acc)
    squares[...] = jnp.zeros_like(squares)
    own_places = places[pl.ds(expert, 1), :]
    pick_ref[...] = (own_places == iota((SLOTS, 256), 0).astype(F32)).astype(BF)

    pl.semaphore_wait(barrier, 25 + 3 * c)

    def gather(buf, ny, w, part, device, sems, aside, work, mixed):
        (
            p_send, p_in, o_send, z_send, z_in, ring, up_in, down_in, y_send, y_in, x_send, l_in,
            r_in, ll_in, rr_in, s_send, s_in,
        ) = sems
        size = buf.shape[4]
        first, second = pl.ds(0, part), pl.ds(part, size - part)
        flat = x * ny + w
        own = buf.at[z, x, w, c]

        def put(ref, send, recv, to):
            copy(ref, ref, send, recv, *to).start()

        def near(n, core):
            return device(lax.rem(z + n + 8, 8), x, w, core)

        def to_plane(d):
            f = lax.rem(flat + d, 4 * ny)
            put(own.at[first], p_send, p_in.at[flat * 2 + c], device(z, f // ny, lax.rem(f, ny), 0))

        @pl.when(c == 1)
        def _():
            put(own.at[first], o_send, p_in.at[flat * 2 + 1], device(z, x, w, 0))

        @pl.when(c == 0)
        def _():
            put(own.at[second], o_send, z_in.at[z * 2], device(z, x, w, 1))

        for n in (1, -1, 2, -2, 3, -3, 4):
            put(own.at[second], z_send, z_in.at[z * 2 + c], near(n, 1))
        for d in range(1, 4 * ny):
            to_plane(d)

        def share(b, ref):
            put(ref, s_send, s_in.at[b], device(z, x, w, 1 - c))

        def share_near(core, rows):
            for i in range(1, ny):
                share(z, buf.at[z, x, lax.rem(w + i, ny), :, rows])
            share(z, buf.at[z, x, w, core, rows])

        def wait_plane(sem, rows, full):
            blocks = buf.reshape(64 * ny, size, 128)
            wait_bytes(blocks.at[pl.ds(0, 8 * ny if full else 8 * ny - 1), rows], sem)

        def finish(n, rows):
            for b in step_planes(n):
                wait_plane(s_in.at[b], rows, n > 0)
            work(step_planes(n))

        @pl.when(c == 0)
        def _():
            def chunk(b, q):
                return buf.at[b, lax.rem(x + (0, 1, 3, 2)[q], 4), :, :, first]

            aside(0, 0)
            for s in range(5):
                b_up, b_down = lax.rem(z + 8 - s, 8), lax.rem(z + s, 8)
                for q in range(4):
                    up_now, down_now = s < 4 or q < 2, s < 4 or q >= 2
                    if s == 0:
                        xx = lax.rem(x + (0, 1, 3, 2)[q], 4)
                        for i in range(ny):
                            ww = lax.rem(w + i, ny)
                            for core in range(2):
                                if q or i or core:
                                    wait_bytes(buf.at[z, xx, ww, core, first], p_in.at[(xx * ny + ww) * 2 + core])
                    if s > 0 and up_now:
                        wait_bytes(chunk(b_up, q), up_in.at[s - 1, q])
                    if s < 3 or (s == 3 and q < 2):
                        put(chunk(b_up, q), ring.at[0], up_in.at[s, q], near(1, 0))
                    if s > 0 and down_now:
                        wait_bytes(chunk(b_down, q), down_in.at[s - 1, q])
                    if s < 3 or (s == 3 and q >= 2):
                        put(chunk(b_down, q), ring.at[1], down_in.at[s, q], near(-1, 0))
                    if s == 0 and q == 0:
                        share_near(0, first)
                    elif s == 0 or up_now:
                        share(b_up, chunk(b_up, q))
                    if s > 0 and down_now:
                        share(b_down, chunk(b_down, q))
                if s < 4:
                    aside(0, s + 1)
                if s == 3 and mixed:
                    finish(0, second)
            for n in range(1 if mixed else 0, 5):
                finish(n, second)

            def ring_sent(n, _):
                for way in range(2):
                    wait_bytes(chunk(n, 0), ring.at[way])
                    wait_bytes(chunk(n, 0), ring.at[way])
                return 0

            lax.fori_loop(0, 7, ring_sent, 0)
            for n in range(8):
                wait_plane(s_send, first, n > 0)
            wait_bytes(own.at[second], o_send)

        @pl.when(c == 1)
        def _():
            left, right = device(z, lax.rem(x + 3, 4), w, 1), device(z, lax.rem(x + 1, 4), w, 1)
            lx, rx, ox = lax.rem(x + 3, 4), lax.rem(x + 1, 4), lax.rem(x + 2, 4)

            def along_z(n):
                for b in step_planes(n):
                    for core in range(2):
                        if n or core == 0:
                            wait_bytes(buf.at[b, x, w, core, second], z_in.at[b * 2 + core])
                    line = buf.at[b, x, w, :, second]
                    for i in range(1, ny):
                        put(line, y_send, y_in.at[b], device(z, x, lax.rem(w + i, ny), 1))

            def along_y(n):
                for b in step_planes(n):
                    wait_bytes(buf.at[b, x, pl.ds(0, ny - 1), :, second], y_in.at[b])
                    face = buf.at[b, x, :, :, second]
                    put(face, x_send, l_in.at[b], right)
                    put(face, x_send, r_in.at[b], left)
                    if n:
                        share(b, face)
                    else:
                        share_near(1, second)

            def along_x(n):
                for b in step_planes(n):
                    face = buf.at[b, lx, :, :, second]
                    wait_bytes(face, l_in.at[b])
                    put(buf.at[b, lx, pl.ds(0, ny // 2), :, second], x_send, ll_in.at[b], right)
                    other = buf.at[b, rx, :, :, second]
                    wait_bytes(other, r_in.at[b])
                    put(buf.at[b, rx, pl.ds(ny // 2, ny // 2), :, second], x_send, rr_in.at[b], left)
                    share(b, face)
                    share(b, other)

            def opposite(n):
                for b in step_planes(n):
                    wait_bytes(buf.at[b, ox, pl.ds(0, ny // 2), :, second], ll_in.at[b])
                    wait_bytes(buf.at[b, ox, pl.ds(ny // 2, ny // 2), :, second], rr_in.at[b])
                    share(b, buf.at[b, ox, :, :, second])

            aside(1, 0)
            along_z(0)
            along_z(1)
            along_y(0)
            for n in (2, 3, 4):
                along_z(n)
            aside(1, 1)
            along_y(1)
            along_y(2)
            aside(1, 2)
            along_y(3)
            along_y(4)
            along_x(0)
            along_x(1)
            aside(1, 3)
            for n in (2, 3, 4):
                along_x(n)
            for n in range(5):
                opposite(n)
                if mixed and n:
                    finish(n - 1, first)
            for n in range(4 if mixed else 0, 5):
                finish(n, first)

            def line_sent(n, _):
                wait_bytes(buf.at[n, x, pl.ds(0, ny - 1), :, second], y_send)
                wait_bytes(buf.at[n, pl.ds(0, 3), :, :, second], x_send)
                return 0

            lax.fori_loop(0, 8, line_sent, 0)
            for n in range(8):
                wait_plane(s_send, second, n > 0)
            wait_bytes(own.at[first], o_send)

        def plane_sent(d, _):
            wait_bytes(own.at[first], p_send)
            return 0

        def line_sent(d, _):
            wait_bytes(own.at[second], z_send)
            return 0

        lax.fori_loop(1, 4 * ny, plane_sent, 0)
        lax.fori_loop(1, 8, line_sent, 0)

    def step_planes(s):
        if s in (0, 4):
            return [lax.rem(z + s, 8)]
        return [lax.rem(z + 8 - s, 8), lax.rem(z + s, 8)]

    def prepare(b, _):
        gains = padded([gain_ref[:, lane_tile(b * 7 + j)] for j in range(7)])
        routers = padded([router_ref[:, lane_tile(b * 7 + j)].astype(F32) for j in range(7)])
        for j in range(8):
            part = (routers[j] * gains[j]).astype(BF)
            fused[320:336, lane_tile(b * 8 + j)] = jnp.concatenate([part, jnp.zeros_like(part)], axis=0)

        def strip(n, _):
            r = pl.ds(pl.multiple_of(n * 32, 32), 32)
            for src, first in ((gate, 0), (up, SLOTS)):
                tiles = padded([src[r, lane_tile(b * 7 + j)] for j in range(7)])
                to = pl.ds(pl.multiple_of(first + n * 32, 32), 32)
                for j in range(8):
                    fused[to, lane_tile(b * 8 + j)] = (tiles[j].astype(F32) * gains[j]).astype(BF)
            tiles = padded([down[r, lane_tile(b * 7 + j)] for j in range(7)])
            for j in range(8):
                cut[r, lane_tile(b * 8 + j)] = tiles[j]
            return 0

        lax.fori_loop(0, 5, strip, 0)
        return 0

    def turn(b):
        def part(k, _):
            block = rows_in[b, :, :, :, pl.ds(pl.multiple_of(k * 16, 16), 16), :]
            block = jnp.swapaxes(block.reshape(16, 16, 128), 0, 1)
            for j in range(16):
                n = 2 * (lax.rem(k, 4) * 16 + j) + k // 4
                rows[b, :, lane_tile(n)] = block[j]
            return 0

        lax.fori_loop(0, 8, part, 0)

    def row_aside(core, n):
        if n == 0:
            loaded("gain", "router", "gate", "up", "down")
        bounds = ((0, 2, 3, 5, 7, 8), (0, 3, 5, 7, 8))[core]
        lax.fori_loop(bounds[n], bounds[n + 1], prepare, 0)

    def row_work(planes):
        for b in planes:
            turn(b)

    def row_device(dz, dx, dw, core):
        return pool, rank_of(dz, dx, dw, core)

    gather(rows_in, 2, yh, 48, row_device, gather_sems[:17], row_aside, row_work, False)

    loaded("weight", "residual")
    projected = lax.dot_general(
        weight[...], rows[...].reshape(128, 16384), (((1,), (1,)), ((), ())),
        preferred_element_type=F32,
    )
    hstate = (residual[...].astype(F32) + projected).astype(BF).astype(F32)
    states[z, x, yh * 2 + pool, c] = jnp.concatenate(
        [hstate, jnp.zeros((8, 128), F32)], axis=0
    ).astype(BF)

    def state_work(planes):
        for b in planes:
            k = pl.ds(pl.multiple_of(b * 1024, 1024), 1024)
            for p in range(2):
                part = jnp.concatenate(
                    [states[b, n // 2, (n % 2) * 2 + p].reshape(128, 128) for n in range(8)], axis=0
                )
                lanes = slice(p * 128, p * 128 + 128)
                acc[:, lanes] += dot(fused[:, k], part)
                wide = part.astype(F32)
                squares[:, lanes] += jnp.sum((wide * wide).reshape(128, 8, 128), axis=0)

    def state_device(dz, dx, dw, core):
        return lax.rem(dw, 2), rank_of(dz, dx, dw // 2, core)

    gather(
        states, 4, yh * 2 + pool, 16, state_device, gather_sems[17:], lambda core, n: None, state_work,
        True,
    )

    pick = pick_ref[...]
    members = (places[...] >= 0.0).astype(F32)
    inv = lax.rsqrt(jnp.sum(squares[...], axis=0, keepdims=True) * (1.0 / 7168) + EPSILON)
    chosen = jax.nn.sigmoid(acc[320:328, :] * inv)
    named = jnp.where(members > 0.5, chosen, 0.0)
    whole = jnp.sum(named, axis=0, keepdims=True)
    row_share = jnp.sum(jnp.where(rows8 == expert, named, 0.0), axis=0, keepdims=True) / whole
    hidden_t = (jax.nn.silu(acc[0:160, :] * inv) * (acc[160:320, :] * inv)).astype(BF)
    hidden = lax.dot_general(
        pick, hidden_t, (((1,), (1,)), ((), ())), preferred_element_type=F32
    ).astype(BF)
    share = jnp.sum(jnp.where(pick.astype(F32) > 0.5, row_share, 0.0), axis=1, keepdims=True)

    def product(core, g, i):
        b = 4 * g + 2 * core + i
        k = pl.ds(pl.multiple_of(b * 1024, 1024), 1024)
        sums = (dot(hidden, cut[:, k]) * share).astype(BF)
        for j in range(8):
            partial[core, i, g, j] = sums[:, j * 128 : j * 128 + 128]

    def for_other(g, i):
        product(1 - c, g, i)
        copy(
            partial.at[1 - c, i, g], from_core.at[i, g], c_send, c_recv.at[2 * i + g], pool, sibling
        ).start()

    def send_sums(g, i):
        wait_bytes(from_core.at[i, g], c_recv.at[2 * i + g])

        def one(j, _):
            to = g * 8 + j
            both = (partial[c, i, g, j].astype(F32) + from_core[i, g, j].astype(F32)).astype(BF)

            @pl.when(to == spot)
            def _():
                from_group[i, to] = both

            @pl.when(to != spot)
            def _():
                to_group[i, to] = both
                copy(
                    to_group.at[i, to], from_group.at[i, spot], r_send, r_recv.at[i], pool,
                    member(to, c),
                ).start()

            return 0

        lax.fori_loop(0, 8, one, 0)

    parts = ((0, 0), (1, 0), (0, 1), (1, 1))
    for_other(*parts[0])
    for_other(*parts[1])
    product(c, *parts[0])
    for n in range(4):
        if n < 2:
            for_other(*parts[n + 2])
        if n < 3:
            product(c, *parts[n + 1])
        send_sums(*parts[n])

    for i in range(2):
        wait_bytes(from_group.at[i, pl.ds(0, 15)], r_recv.at[i])
        total = from_group[i, 0].astype(F32)
        for s in range(1, 16):
            total += from_group[i, s].astype(F32)
        spread = lax.dot_general(
            total.astype(BF), pick, (((0,), (0,)), ((), ())), preferred_element_type=F32
        ).astype(BF)
        for p in range(2):
            for core in range(2):
                to_rows[i, p, core] = spread[core * 64 : core * 64 + 64, p * 128 : p * 128 + 128]
        for p in range(2):
            for core in range(2):
                r = rank_of(4 * zb + 2 * c + i, x, yh, core)
                src, dst = to_rows.at[i, p, core], from_experts.at[expert]
                here = is_self(p, r)

                @pl.when(here)
                def _():
                    pltpu.make_async_copy(src, dst, d_recv).start()

                @pl.when(jnp.logical_not(here))
                def _():
                    copy(src, dst, d_send, d_recv, p, r).start()

    wait_bytes(from_experts, d_recv)
    sums = from_experts[0].astype(F32)
    for e in range(1, 8):
        sums += from_experts[e].astype(F32)
    out_ref[...] = (hstate + sums[0:56]).astype(BF)

    wait_bytes(from_core, c_send)
    wait_bytes(from_group.at[:, pl.ds(0, 15)], r_send)
    wait_bytes(from_experts.at[pl.ds(0, 7)], d_send)

    @pl.when(jnp.logical_not(same))
    def _():
        wait_bytes(from_experts.at[0], d_send)


def local(
    queries, cache_keys, cache_values, new_keys, new_values, lengths, residual, out_weight,
    norm_gain, router_weight, routes, gate_tiles, up_tiles, down_tiles,
):
    dma = pltpu.SemaphoreType.DMA
    vmem = pltpu.VMEM

    def gather_sems(ny):
        return [
            dma, dma((8 * ny,)), dma, dma, dma((16,)), dma((2,)), dma((4, 4)), dma((4, 4)), dma,
            dma((8,)), dma, dma((8,)), dma((8,)), dma((8,)), dma((8,)), dma, dma((8,)),
        ]

    return pl.pallas_call(
        layer_kernel,
        out_shape=jax.ShapeDtypeStruct((56, 128), BF),
        in_specs=[
            ANY, ANY, ANY, ANY, ANY, ANY, ANY, ANY, ANY, ANY, ANY, ANY, ANY, ANY,
        ],
        out_specs=VM,
        scratch_shapes=[
            vmem((1, 256), BF),
            vmem((1, 256), BF),
            vmem((1, 1), jnp.int32),
            vmem((1, 7168), F32),
            vmem((8, 7168), BF),
            vmem((3, 256), jnp.int32),
            vmem((64, 256), BF),
            vmem((2048, 256), BF),
            vmem((2048, 256), BF),
            vmem((56, 128), BF),
            vmem((56, 16384), BF),
            vmem((SLOTS, 7168), BF),
            vmem((SLOTS, 7168), BF),
            vmem((SLOTS, 7168), BF),
            vmem((336, 8192), BF),
            vmem((SLOTS, 8192), BF),
            vmem((8, 4, 2, 2, 128, 128), BF),
            vmem((8, 16, 16384), BF),
            vmem((8, 4, 4, 2, 64, 128), BF),
            vmem((336, 256), F32),
            vmem((8, 256), F32),
            vmem((SLOTS, 256), BF),
            vmem((2, 2, 2, 8, SLOTS, 128), BF),
            vmem((2, 2, 8, SLOTS, 128), BF),
            vmem((2, 16, SLOTS, 128), BF),
            vmem((2, 16, SLOTS, 128), BF),
            vmem((2, 2, 2, 64, 128), BF),
            vmem((8, 64, 128), BF),
            vmem((8, 256), F32),
            dma((14,)),
            dma, dma((4,)), dma, dma((2,)), dma, dma,
            *gather_sems(2),
            *gather_sems(4),
        ],
        compiler_params=pltpu.CompilerParams(
            collective_id=0, has_side_effects=True, vmem_limit_bytes=56 * 2**20
        ),
        name="decode_layer",
    )(
        queries, cache_keys, cache_values, new_keys, new_values, lengths.reshape(1, 1), residual.T, out_weight,
        norm_gain.reshape(1, 7168), router_weight.T, routes.T, jnp.swapaxes(gate_tiles, 1, 2),
        jnp.swapaxes(up_tiles, 1, 2), down_tiles,
    ).T


def solution(mesh):
    return jax.shard_map(
        local,
        mesh=mesh,
        in_specs=(
            P(("pool", "rank"), None, None),
            P(("pool", "rank"), None, None),
            P(("pool", "rank"), None, None),
            P(("pool", "rank"), None),
            P(("pool", "rank"), None),
            P(("pool", "rank")),
            P("pool", "rank"),
            P("rank", None),
            P(),
            P(),
            P(),
            P(("pool", "rank"), None, None),
            P(("pool", "rank"), None, None),
            P(("pool", "rank"), None, None),
        ),
        out_specs=P("pool", "rank"),
        check_vma=False,
    )
```
